32 devices in a mesh: walk: 8 (over z, x), chol: 4 (over y, core).
Axes of the slice: x: 2, y: 2, z: 4, core: 2. Of those that a mesh axis runs over, the one named last changes fastest.
Arguments:
- walkers: bfloat16 [48, 2048, 128], P('walk', 'chol'), may hold values from -6 to 6
- inv_intersection: bfloat16 [48, 128, 128], P('walk'), may hold values from -0.5 to 0.5
- fields: bfloat16 [48, 8], P('walk', 'chol'), may hold values from -5 to 5
- cholesky: bfloat16 [8, 256, 2048], P('chol'), may hold values from -0.125 to 0.125
- trial_rows: bfloat16 [256, 128], replicated, may hold values from -0.33007812 to 0.33007812
- counts: int32 [8], replicated, may hold values from 1 to 6, as said below
- partner: int32 [8], replicated, may hold values from 0 to 7, as said below
Outputs:
- new_walkers: bfloat16 [32, 256, 128], P('walk', 'chol')
- log_weight: float32 [32], P('walk')
The draws below stay inside these ranges and needn't reach their ends.
Inputs may be any that keep to these rules, and one draw needn't show every extreme that they name: `counts`: of w and partner[w], exactly one holds more than 4 walkers, and the other holds at most 8 minus that count; some walk index holds exactly 6 walkers. partner[partner[w]] = w, and partner[w] differs from w in exactly one bit.
All inputs are finite; a program needn't handle non-finite values.
Results may differ from the reference program's by a relative error of at most 0.0075.
Values may be sent and summed in bfloat16 or wider, within the bound.
A program may use at most 64 MiB of HBM per device.

```python
import jax
import jax.numpy as jnp
from jax import lax

NORB = 2048
NOCC = 128
NCHOL = 8
ROWS_DEV = 64
R = 256
LIVE = 4
MOVE = 2
SLOTS = 6
WALK_DEVS = 8
WALKERS = 48
BALANCED = 32
N_CHOL = 4


def pairing(key):
    base_key = jax.random.fold_in(key, 11)
    key_order, key_coin, key_move, key_count = jax.random.split(base_key, 4)
    key_label = jax.random.fold_in(base_key, 23)
    bit_count = WALK_DEVS.bit_length() - 1
    device_ids = jnp.arange(WALK_DEVS, dtype=jnp.int32)
    translate = jax.random.randint(key_label, (), 0, WALK_DEVS).astype(jnp.int32)
    labels = jnp.bitwise_xor(device_ids, translate)
    order = jax.random.permutation(key_order, bit_count).astype(jnp.int32)
    chosen_bit = jnp.zeros((WALK_DEVS,), jnp.int32) - 1
    taken_mask = jnp.int32(0)
    for level in range(bit_count):
        level_bit = order[level]
        group_ids = jnp.bitwise_and(labels, taken_mask)
        level_coin = jax.random.randint(jax.random.fold_in(base_key, 100 + level), (WALK_DEVS,), 0, 4)[group_ids]
        if level == bit_count - 1:
            settle = chosen_bit < 0
        elif level == 0:
            settle = (chosen_bit < 0) & (level_coin == 0)
        else:
            settle = (chosen_bit < 0) & (level_coin >= 2)
        chosen_bit = jnp.where(settle, level_bit, chosen_bit)
        taken_mask = jnp.bitwise_or(taken_mask, jnp.left_shift(jnp.int32(1), level_bit))
    partner = jnp.bitwise_xor(device_ids, jnp.left_shift(jnp.int32(1), chosen_bit))
    pair_low = jnp.minimum(device_ids, partner)
    pair_high = jnp.maximum(device_ids, partner)
    last_id = WALK_DEVS - 1
    first_pair = pair_low == 0
    last_pair = pair_high == last_id
    coin_flip = jax.random.randint(key_coin, (WALK_DEVS,), 0, 2)
    surplus = (coin_flip[pair_low] == 1) == (device_ids == pair_low)
    surplus = jnp.where(first_pair, device_ids != 0, jnp.where(last_pair, device_ids != last_id, surplus))
    moved_count = jax.random.randint(key_move, (WALK_DEVS,), 1, MOVE + 1)[pair_low]
    moved_count = jnp.where(first_pair | last_pair, MOVE, moved_count)
    deficit_count = jax.random.randint(key_count, (WALK_DEVS,), 0, 1 << 20) % (LIVE - moved_count) + 1
    counts = jnp.where(surplus, LIVE + moved_count, deficit_count)
    return (counts.astype(jnp.int32), partner.astype(jnp.int32))


def draw_counts(key, part):
    return pairing(key)[0]


def draw_partner(key, part):
    return pairing(key)[1]


def block_levels(own_key, dims, pieces, low, high):
    def one(position, blocks):
        steps = jax.random.uniform(jax.random.fold_in(jax.random.fold_in(own_key, 6), position), (blocks,), jnp.float32, low / len(pieces), high / len(pieces))
        return jnp.repeat(jnp.exp(steps), dims[position] // blocks).reshape((-1,) + (1,) * (len(dims) - position - 1))

    factor_of = one(*pieces[0])
    for cut in pieces[1:]:
        factor_of = factor_of * one(*cut)
    return factor_of


def gaussian(own_key, dims, width, most, cuts=(), kind=jnp.bfloat16):
    array = jax.random.normal(own_key, dims, jnp.float32) * width
    if len(cuts) > 0:
        array = block_levels(own_key, dims, cuts, -0.22, 0.18) * array
    return jnp.clip(array, min=-most, max=most).astype(kind)


def setup_inputs(seed: int = 0) -> dict:
    key_list = jax.random.split(jax.random.key(seed), 8)
    walkers = gaussian(key_list[0], (WALKERS, NORB, NOCC), 1.0, 6.0, ((0, 8), (1, 4)))
    inv_intersection = gaussian(key_list[1], (WALKERS, NOCC, NOCC), NOCC ** -0.5, 0.5, ((0, 8),))
    fields = gaussian(key_list[2], (WALKERS, NCHOL), 1.0, 5.0, ((0, 8), (1, 4)))
    cholesky = gaussian(key_list[3], (NCHOL, R, NORB), NORB ** -0.5, 0.125, ((0, 4),))
    trial_rows = gaussian(key_list[4], (R, NOCC), (10.0 / (R * NOCC) ** 0.5), 0.33007812)
    counts = draw_counts(jax.random.fold_in(key_list[7], 71), 0)
    partner = draw_partner(jax.random.fold_in(key_list[7], 71), 0)
    return {"walkers": walkers, "inv_intersection": inv_intersection, "fields": fields, "cholesky": cholesky, "trial_rows": trial_rows, "counts": counts, "partner": partner}


STEP_ROOT = 0.1


def expand_mask(mask_in, target):
    return mask_in.reshape(mask_in.shape + (1,) * (target.ndim - mask_in.ndim))


def select_slots(own_part, arriving, own_mask, incoming):
    arrived = jnp.zeros_like(own_part)
    for slot_num in range(MOVE):
        flag = incoming[:, :, slot_num]
        arrived = jnp.where(expand_mask(flag, own_part), arriving[:, slot_num:slot_num + 1], arrived)
    return jnp.where(expand_mask(own_mask, own_part), own_part, arrived)


def reference(walkers, inv_intersection, fields, cholesky, trial_rows, counts, partner):
    grouped = walkers.reshape(WALK_DEVS, SLOTS, NORB, NOCC)
    grouped_minv = inv_intersection.reshape(WALK_DEVS, SLOTS, NOCC, NOCC)
    grouped_fields = fields.reshape(WALK_DEVS, SLOTS, NCHOL)
    mate_count = counts[partner]
    arriving_count = jnp.maximum(mate_count - LIVE, 0)
    slot_ids = jnp.arange(LIVE, dtype=jnp.int32)
    own_mask = slot_ids[None, :] < jnp.minimum(counts, LIVE)[:, None]
    move_ids = jnp.arange(MOVE, dtype=jnp.int32)
    incoming = (slot_ids[None, :, None] - counts[:, None, None] == move_ids[None, None, :]) & (move_ids[None, None, :] < arriving_count[:, None, None])
    live = own_mask | jnp.any(incoming, axis=2)
    phi = select_slots(grouped[:, :LIVE], grouped[partner, LIVE:], own_mask, incoming)
    minv = select_slots(grouped_minv[:, :LIVE], grouped_minv[partner, LIVE:], own_mask, incoming)
    field_vals = select_slots(grouped_fields[:, :LIVE], grouped_fields[partner, LIVE:], own_mask, incoming)
    chol_wide = cholesky.astype(jnp.float32)
    trial_wide = trial_rows.astype(jnp.float32)

    def one_group(inputs):
        phi_group, minv_group, field_group, live_group = inputs
        products = jnp.einsum('grk,wkn->wgrn', chol_wide, phi_group.astype(jnp.float32))
        weighted = jnp.einsum('rb,wab->wra', trial_wide, minv_group.astype(jnp.float32))
        force_bias = -STEP_ROOT * jnp.einsum('wgrn,wrn->wg', products, weighted)
        field_wide = field_group.astype(jnp.float32)
        shifted = STEP_ROOT * (field_wide - force_bias)
        increment = jnp.einsum('wg,wgrn->wrn', shifted, products)
        log_terms = jnp.sum(field_wide * force_bias - 0.5 * force_bias * force_bias, axis=1)
        window = phi_group.reshape(LIVE, N_CHOL, NORB // N_CHOL, NOCC)[:, :, :ROWS_DEV].reshape(LIVE, R, NOCC)
        live_wide = live_group.astype(jnp.float32)
        new_rows = (live_wide[:, None, None] * (window.astype(jnp.float32) + increment)).astype(jnp.bfloat16)
        return new_rows, live_wide * log_terms

    new_rows, log_terms = lax.map(one_group, (phi, minv, field_vals, live))
    return new_rows.reshape(BALANCED, R, NOCC), log_terms.reshape(BALANCED)
```

```python
import functools

import jax
import jax.numpy as jnp
from jax import lax
from jax.experimental import pallas as pl
from jax.experimental.pallas import tpu as pltpu
from jax.sharding import PartitionSpec as P

LIVE = 4
MOVE = 2
STEP_ROOT = 0.1
LOG_ROWS = 8
TAIL = 2 * LOG_ROWS
MESH = pl.DeviceIdType.MESH


def pick(flag, chosen, other):
    mask = jnp.broadcast_to(flag.astype(jnp.int32), chosen.shape) > 0
    return jnp.where(mask, chosen, other)


def kernel(
    chol_count,
    bit_count,
    walkers,
    minv_in,
    fields,
    chol_in,
    trial_in,
    counts,
    partner,
    new_out,
    log_out,
    phi,
    chol,
    minv,
    trial,
    prod,
    weighted,
    terms,
    logs,
    mine,
    sib_out,
    sib_in,
    far_out,
    far_in,
    moved_out,
    moved_in,
    load_sem,
    near_sem,
    ahead_send,
    ahead_recv,
    pass_send,
    pass_recv,
    sib_send,
    sib_recv,
    far_send,
    far_recv,
    moved_send,
    moved_recv,
):
    slots, depth, occ = walkers.shape
    vectors, rows, _ = chol_in.shape
    own_rows = rows // chol_count
    half = chol_count // 2
    walk = lax.axis_index("walk")
    me = lax.axis_index("chol")
    high, low = me // 2, me % 2
    sibling = 2 * high + 1 - low
    far_ids = [2 * lax.rem(high + step, half) + low for step in range(1, half)]
    from_high = [lax.rem(high - step + half, half) for step in range(1, half)]
    mates = [jnp.bitwise_xor(walk, 1 << bit) for bit in range(bit_count)]

    loads = [
        pltpu.make_async_copy(walkers, phi.at[:, me], load_sem.at[0]),
        pltpu.make_async_copy(chol_in, chol, load_sem.at[1]),
        pltpu.make_async_copy(minv_in, minv, load_sem.at[2]),
        pltpu.make_async_copy(trial_in, trial, load_sem.at[3]),
    ]
    for load in loads:
        load.start()

    barrier = pltpu.get_barrier_semaphore()
    peers = [{"chol": sibling}] + [{"chol": far} for far in far_ids] + [{"walk": mate} for mate in mates]
    for peer in peers:
        pl.semaphore_signal(barrier, inc=1, device_id=peer, device_id_type=MESH)
    pl.semaphore_wait(barrier, len(peers))

    def remote(src, dst, send, recv, peer):
        return pltpu.make_async_remote_copy(
            src_ref=src, dst_ref=dst, send_sem=send, recv_sem=recv, device_id=peer, device_id_type=MESH
        )

    order = list(range(LIVE, slots)) + list(range(LIVE))
    ahead = {}
    for slot in order:
        for step in range(half - 1):
            ahead[slot, step] = remote(
                walkers.at[slot],
                phi.at[slot, me],
                ahead_send.at[slot, step],
                ahead_recv.at[slot, step],
                {"chol": far_ids[step]},
            )
            ahead[slot, step].start()
    near = remote(walkers, phi.at[:, me], near_sem.at[0], near_sem.at[1], {"chol": sibling})
    near.start()

    for load in loads[2:]:
        load.wait()
    for slot in range(slots):
        weighted[slot] = lax.dot_general(
            trial[...], minv[slot], (((1,), (1,)), ((), ())), preferred_element_type=jnp.float32
        )
    for load in loads[:2]:
        load.wait()
    near.wait_recv()

    def chol_half(index):
        columns = pl.ds(pl.multiple_of(index * 2 * depth, 2 * depth), 2 * depth)
        return chol[:, :, columns].reshape(vectors * rows, 2 * depth)

    def phi_half(slot, index):
        return phi[slot, pl.ds(2 * index, 2)].reshape(2 * depth, occ)

    @pl.loop(0, slots // 2)
    def _(pair):
        both = jnp.concatenate([phi_half(2 * pair, high), phi_half(2 * pair + 1, high)], axis=1)
        result = jnp.dot(chol_half(high), both, preferred_element_type=jnp.float32)
        prod[2 * pair] = result[:, :occ]
        prod[2 * pair + 1] = result[:, occ:]

    field_wide = fields[...].astype(jnp.float32)

    def multiply(slot):
        passed = []
        for step in range(half - 1):
            ahead[slot, step].wait_recv()
            block = phi.at[slot, 2 * from_high[step] + low]
            passed.append(
                remote(block, block, pass_send.at[slot, step], pass_recv.at[slot, step], {"chol": sibling})
            )
            passed[step].start()
        total = prod[slot]
        for step in range(half - 1):
            passed[step].wait_recv()
            total += jnp.dot(
                chol_half(from_high[step]),
                phi_half(slot, from_high[step]),
                preferred_element_type=jnp.float32,
            )
        total = total.reshape(vectors, rows, occ)
        increment = jnp.zeros((rows, occ), jnp.float32)
        weight = jnp.zeros((1, 1), jnp.float32)
        for vector in range(vectors):
            force_bias = -STEP_ROOT * jnp.sum(total[vector] * weighted[slot], keepdims=True)
            field = field_wide[slot : slot + 1, vector : vector + 1]
            increment += (STEP_ROOT * (field - force_bias)) * total[vector]
            weight += field * force_bias - 0.5 * force_bias * force_bias
        terms[slot] = increment.reshape(chol_count, own_rows, occ)
        logs[slot] = jnp.broadcast_to(weight, (LOG_ROWS, occ))
        for index in range(half):
            sib_out[slot, pl.ds(index * own_rows, own_rows)] = terms[slot, 2 * index + 1 - low]
        sib_out[slot, pl.ds(half * own_rows, LOG_ROWS)] = logs[slot]
        copy = remote(
            sib_out.at[slot], sib_in.at[slot], sib_send.at[slot], sib_recv.at[slot], {"chol": sibling}
        )
        copy.start()
        return passed, copy

    def chip_sum(slot, index):
        start = pl.multiple_of(index * own_rows, own_rows)
        return terms[slot, 2 * index + low] + sib_in[slot, pl.ds(start, own_rows)]

    def add_chip(slot, copy):
        copy.wait_recv()
        weight = logs[slot] + sib_in[slot, pl.ds(half * own_rows, LOG_ROWS)]
        logs[slot] = weight
        coarse = weight.astype(jnp.bfloat16).astype(jnp.float32)
        tail = jnp.concatenate([coarse, weight - coarse], axis=0).astype(jnp.bfloat16)
        copies = []
        for step in range(half - 1):
            far_out[slot, step, pl.ds(0, own_rows)] = chip_sum(slot, lax.rem(high + step + 1, half)).astype(
                jnp.bfloat16
            )
            far_out[slot, step, pl.ds(own_rows, TAIL)] = tail
            copies.append(
                remote(
                    far_out.at[slot, step],
                    far_in.at[slot, step],
                    far_send.at[slot, step],
                    far_recv.at[slot, step],
                    {"chol": far_ids[step]},
                )
            )
            copies[step].start()
        mine[slot] = chip_sum(slot, high) + phi[slot, me, pl.ds(0, own_rows)].astype(jnp.float32)
        return copies

    def split_log(tail):
        return tail[:LOG_ROWS] + tail[LOG_ROWS:]

    def finish(slot, copies):
        result, weight = mine[slot], logs[slot]
        for step in range(half - 1):
            copies[step].wait_recv()
            result += far_in[slot, step, pl.ds(0, own_rows)].astype(jnp.float32)
            weight += split_log(far_in[slot, step, pl.ds(own_rows, TAIL)].astype(jnp.float32))
        if slot < LIVE:
            mine[slot] = result
            logs[slot] = weight
        else:
            start = (slot - LIVE) * (own_rows + TAIL)
            coarse = weight.astype(jnp.bfloat16).astype(jnp.float32)
            moved_out[pl.ds(start, own_rows)] = result.astype(jnp.bfloat16)
            moved_out[pl.ds(start + own_rows, TAIL)] = jnp.concatenate(
                [coarse, weight - coarse], axis=0
            ).astype(jnp.bfloat16)

    moved = [
        remote(moved_out, moved_in.at[bit], moved_send.at[bit], moved_recv.at[bit], {"walk": mates[bit]})
        for bit in range(bit_count)
    ]
    sent, near_copies, far_copies = [near] + list(ahead.values()), {}, {}

    def later(position):
        if position - 1 >= 0 and position - 1 < slots:
            slot = order[position - 1]
            far_copies[slot] = add_chip(slot, near_copies[slot])
        if position - 2 >= 0:
            slot = order[position - 2]
            finish(slot, far_copies[slot])
            if slot == slots - 1:
                for copy in moved:
                    copy.start()

    for position in range(slots):
        slot = order[position]
        passed, near_copies[slot] = multiply(slot)
        sent += passed
        later(position)
    later(slots)
    later(slots + 1)

    for copy in sent + list(near_copies.values()) + sum(far_copies.values(), []):
        copy.wait_send()
    for copy in moved:
        copy.wait()

    mate = partner[walk]
    own_count = counts[walk]
    arriving = jnp.maximum(counts[mate] - LIVE, 0)
    distance = jnp.bitwise_xor(mate, walk)

    def arrived(offset, size):
        value = moved_in[0, pl.ds(offset, size)].astype(jnp.float32)
        for bit in range(1, bit_count):
            other = moved_in[bit, pl.ds(offset, size)].astype(jnp.float32)
            value = pick(distance == 1 << bit, other, value)
        return value

    came_rows = [arrived(move * (own_rows + TAIL), own_rows) for move in range(MOVE)]
    came_logs = [split_log(arrived(move * (own_rows + TAIL) + own_rows, TAIL)) for move in range(MOVE)]
    for slot in range(LIVE):
        result, weight = jnp.zeros((own_rows, occ), jnp.float32), jnp.zeros((LOG_ROWS, occ), jnp.float32)
        for move in range(MOVE):
            flag = (slot - own_count == move) & (move < arriving)
            result = pick(flag, came_rows[move], result)
            weight = pick(flag, came_logs[move], weight)
        flag = slot < jnp.minimum(own_count, LIVE)
        new_out[slot] = pick(flag, mine[slot], result).astype(jnp.bfloat16)
        weight = pick(flag, logs[slot], weight)
        log_out[slot] = weight[0, 0]


def shards(walkers, inv_intersection, fields, cholesky, trial_rows, counts, partner):
    chol_count = lax.axis_size("chol")
    bit_count = lax.axis_size("walk").bit_length() - 1
    slots, depth, occ = walkers.shape
    vectors, rows, orbitals = cholesky.shape
    own_rows = rows // chol_count
    half = chol_count // 2
    others = half - 1
    bf16, f32 = jnp.bfloat16, jnp.float32
    dma = pltpu.SemaphoreType.DMA
    anywhere = pl.BlockSpec(memory_space=pl.ANY)
    vmem = pl.BlockSpec(memory_space=pltpu.VMEM)
    smem = pl.BlockSpec(memory_space=pltpu.SMEM)
    return pl.pallas_call(
        functools.partial(kernel, chol_count, bit_count),
        out_shape=(
            jax.ShapeDtypeStruct((LIVE, own_rows, occ), bf16),
            jax.ShapeDtypeStruct((LIVE,), f32),
        ),
        in_specs=[anywhere, anywhere, vmem, anywhere, anywhere, smem, smem],
        out_specs=(vmem, smem),
        scratch_shapes=[
            pltpu.VMEM((slots, chol_count, depth, occ), bf16),
            pltpu.VMEM((vectors, rows, orbitals), bf16),
            pltpu.VMEM((slots, occ, occ), bf16),
            pltpu.VMEM((rows, occ), bf16),
            pltpu.VMEM((slots, vectors * rows, occ), f32),
            pltpu.VMEM((slots, rows, occ), f32),
            pltpu.VMEM((slots, chol_count, own_rows, occ), f32),
            pltpu.VMEM((slots, LOG_ROWS, occ), f32),
            pltpu.VMEM((slots, own_rows, occ), f32),
            pltpu.VMEM((slots, half * own_rows + LOG_ROWS, occ), f32),
            pltpu.VMEM((slots, half * own_rows + LOG_ROWS, occ), f32),
            pltpu.VMEM((slots, others, own_rows + TAIL, occ), bf16),
            pltpu.VMEM((slots, others, own_rows + TAIL, occ), bf16),
            pltpu.VMEM((MOVE * (own_rows + TAIL), occ), bf16),
            pltpu.VMEM((bit_count, MOVE * (own_rows + TAIL), occ), bf16),
            dma((4,)),
            dma((2,)),
            dma((slots, others)),
            dma((slots, others)),
            dma((slots, others)),
            dma((slots, others)),
            dma((slots,)),
            dma((slots,)),
            dma((slots, others)),
            dma((slots, others)),
            dma((bit_count,)),
            dma((bit_count,)),
        ],
        compiler_params=pltpu.CompilerParams(
            collective_id=0, has_side_effects=True, vmem_limit_bytes=48 << 20
        ),
        cost_estimate=pl.CostEstimate(
            flops=2 * slots * vectors * rows * orbitals * occ,
            bytes_accessed=2 * (walkers.size + cholesky.size),
            transcendentals=0,
        ),
    )(walkers, inv_intersection, fields, cholesky, trial_rows, counts, partner)


def solution(mesh):
    in_specs = (
        P("walk", "chol", None),
        P("walk", None, None),
        P("walk", "chol"),
        P("chol", None, None),
        P(),
        P(),
        P(),
    )
    out_specs = (P("walk", "chol", None), P("walk"))
    return jax.shard_map(shards, mesh=mesh, in_specs=in_specs, out_specs=out_specs, check_vma=False)
```

```python
import functools

import jax
import jax.numpy as jnp
from jax import lax
from jax.experimental import pallas as pl
from jax.experimental.pallas import tpu as pltpu
from jax.sharding import PartitionSpec as P

LIVE = 4
MOVE = 2
DEPTH = 3
LAG = 4
STEP_ROOT = 0.1
LOG_ROWS = 8
TAIL = 2 * LOG_ROWS
MESH = pl.DeviceIdType.MESH


def pick(flag, chosen, other):
    mask = jnp.broadcast_to(flag.astype(jnp.int32), chosen.shape) > 0
    return jnp.where(mask, chosen, other)


def kernel(
    chol_count,
    bit_count,
    walkers,
    minv_in,
    fields,
    chol_in,
    trial_in,
    counts,
    partner,
    new_out,
    log_out,
    phi,
    chol,
    minv,
    trial,
    prod,
    weighted,
    terms,
    logs,
    mine,
    sib_out,
    sib_in,
    far_out,
    far_in,
    moved_out,
    moved_in,
    load_sem,
    near_sem,
    ahead_send,
    ahead_recv,
    pass_send,
    pass_recv,
    sib_send,
    sib_recv,
    far_send,
    far_recv,
    moved_send,
    moved_recv,
):
    slots, depth, occ = walkers.shape
    vectors, rows, _ = chol_in.shape
    own_rows = rows // chol_count
    half = chol_count // 2
    walk = lax.axis_index("walk")
    me = lax.axis_index("chol")
    high, low = me // 2, me % 2
    sibling = 2 * high + 1 - low
    far_ids = [2 * lax.rem(high + step, half) + low for step in range(1, half)]
    from_high = [lax.rem(high - step + half, half) for step in range(1, half)]
    mates = [jnp.bitwise_xor(walk, 1 << bit) for bit in range(bit_count)]

    loads = [
        pltpu.make_async_copy(walkers, phi.at[:, me], load_sem.at[0]),
        pltpu.make_async_copy(chol_in, chol, load_sem.at[1]),
        pltpu.make_async_copy(minv_in, minv, load_sem.at[2]),
        pltpu.make_async_copy(trial_in, trial, load_sem.at[3]),
    ]
    for load in loads:
        load.start()

    barrier = pltpu.get_barrier_semaphore()
    peers = [{"chol": sibling}] + [{"chol": far} for far in far_ids] + [{"walk": mate} for mate in mates]
    for peer in peers:
        pl.semaphore_signal(barrier, inc=1, device_id=peer, device_id_type=MESH)
    pl.semaphore_wait(barrier, len(peers))

    def remote(src, dst, send, recv, peer):
        return pltpu.make_async_remote_copy(
            src_ref=src, dst_ref=dst, send_sem=send, recv_sem=recv, device_id=peer, device_id_type=MESH
        )

    order = list(range(LIVE, slots)) + list(range(LIVE))
    ahead = {}
    for slot in order:
        for step in range(half - 1):
            ahead[slot, step] = remote(
                walkers.at[slot],
                phi.at[slot, me],
                ahead_send.at[slot, step],
                ahead_recv.at[slot, step],
                {"chol": far_ids[step]},
            )
    for slot in order[:DEPTH]:
        for step in range(half - 1):
            ahead[slot, step].start()
    near = remote(walkers, phi.at[:, me], near_sem.at[0], near_sem.at[1], {"chol": sibling})
    near.start()

    for load in loads[2:]:
        load.wait()
    for slot in range(slots):
        weighted[slot] = lax.dot_general(
            trial[...], minv[slot], (((1,), (1,)), ((), ())), preferred_element_type=jnp.float32
        )
    for load in loads[:2]:
        load.wait()
    near.wait_recv()

    def chol_half(index):
        columns = pl.ds(pl.multiple_of(index * 2 * depth, 2 * depth), 2 * depth)
        return chol[:, :, columns].reshape(vectors * rows, 2 * depth)

    def phi_half(slot, index):
        return phi[slot, pl.ds(2 * index, 2)].reshape(2 * depth, occ)

    @pl.loop(0, slots // 2)
    def _(pair):
        both = jnp.concatenate([phi_half(2 * pair, high), phi_half(2 * pair + 1, high)], axis=1)
        result = jnp.dot(chol_half(high), both, preferred_element_type=jnp.float32)
        prod[2 * pair] = result[:, :occ]
        prod[2 * pair + 1] = result[:, occ:]

    field_wide = fields[...].astype(jnp.float32)

    def multiply(slot):
        passed = []
        for step in range(half - 1):
            ahead[slot, step].wait_recv()
            block = phi.at[slot, 2 * from_high[step] + low]
            passed.append(
                remote(block, block, pass_send.at[slot, step], pass_recv.at[slot, step], {"chol": sibling})
            )
            passed[step].start()
            following = order.index(slot) + DEPTH
            if following < slots:
                ahead[order[following], step].start()
        total = prod[slot]
        for step in range(half - 1):
            passed[step].wait_recv()
            total += jnp.dot(
                chol_half(from_high[step]),
                phi_half(slot, from_high[step]),
                preferred_element_type=jnp.float32,
            )
        total = total.reshape(vectors, rows, occ)
        increment = jnp.zeros((rows, occ), jnp.float32)
        weight = jnp.zeros((1, 1), jnp.float32)
        for vector in range(vectors):
            force_bias = -STEP_ROOT * jnp.sum(total[vector] * weighted[slot], keepdims=True)
            field = field_wide[vector : vector + 1, slot : slot + 1]
            increment += (STEP_ROOT * (field - force_bias)) * total[vector]
            weight += field * force_bias - 0.5 * force_bias * force_bias
        terms[slot] = increment.reshape(chol_count, own_rows, occ)
        logs[slot] = jnp.broadcast_to(weight, (LOG_ROWS, occ))
        for index in range(half):
            sib_out[slot, pl.ds(index * own_rows, own_rows)] = terms[slot, 2 * index + 1 - low]
        sib_out[slot, pl.ds(half * own_rows, LOG_ROWS)] = logs[slot]
        copy = remote(
            sib_out.at[slot], sib_in.at[slot], sib_send.at[slot], sib_recv.at[slot], {"chol": sibling}
        )
        copy.start()
        return passed, copy

    def chip_sum(slot, index):
        start = pl.multiple_of(index * own_rows, own_rows)
        return terms[slot, 2 * index + low] + sib_in[slot, pl.ds(start, own_rows)]

    def add_chip(slot, copy):
        copy.wait_recv()
        weight = logs[slot] + sib_in[slot, pl.ds(half * own_rows, LOG_ROWS)]
        logs[slot] = weight
        coarse = weight.astype(jnp.bfloat16).astype(jnp.float32)
        tail = jnp.concatenate([coarse, weight - coarse], axis=0).astype(jnp.bfloat16)
        copies = []
        for step in range(half - 1):
            far_out[slot, step, pl.ds(0, own_rows)] = chip_sum(slot, lax.rem(high + step + 1, half)).astype(
                jnp.bfloat16
            )
            far_out[slot, step, pl.ds(own_rows, TAIL)] = tail
            copies.append(
                remote(
                    far_out.at[slot, step],
                    far_in.at[slot, step],
                    far_send.at[slot, step],
                    far_recv.at[slot, step],
                    {"chol": far_ids[step]},
                )
            )
            copies[step].start()
        mine[slot] = chip_sum(slot, high) + phi[slot, me, pl.ds(0, own_rows)].astype(jnp.float32)
        return copies

    def split_log(tail):
        return tail[:LOG_ROWS] + tail[LOG_ROWS:]

    def finish(slot, copies):
        result, weight = mine[slot], logs[slot]
        for step in range(half - 1):
            copies[step].wait_recv()
            result += far_in[slot, step, pl.ds(0, own_rows)].astype(jnp.float32)
            weight += split_log(far_in[slot, step, pl.ds(own_rows, TAIL)].astype(jnp.float32))
        if slot < LIVE:
            mine[slot] = result
            logs[slot] = weight
        else:
            start = (slot - LIVE) * (own_rows + TAIL)
            coarse = weight.astype(jnp.bfloat16).astype(jnp.float32)
            moved_out[pl.ds(start, own_rows)] = result.astype(jnp.bfloat16)
            moved_out[pl.ds(start + own_rows, TAIL)] = jnp.concatenate(
                [coarse, weight - coarse], axis=0
            ).astype(jnp.bfloat16)

    moved = [
        remote(moved_out, moved_in.at[bit], moved_send.at[bit], moved_recv.at[bit], {"walk": mates[bit]})
        for bit in range(bit_count)
    ]
    sent, near_copies, far_copies = [near] + list(ahead.values()), {}, {}

    def later(position):
        if position - 1 >= 0 and position - 1 < slots:
            slot = order[position - 1]
            far_copies[slot] = add_chip(slot, near_copies[slot])
        if 0 <= position - LAG < slots:
            slot = order[position - LAG]
            finish(slot, far_copies[slot])
            if slot == slots - 1:
                for copy in moved:
                    copy.start()

    for position in range(slots):
        slot = order[position]
        passed, near_copies[slot] = multiply(slot)
        sent += passed
        later(position)
    for position in range(slots, slots + LAG):
        later(position)

    for copy in sent + list(near_copies.values()) + sum(far_copies.values(), []):
        copy.wait_send()
    for copy in moved:
        copy.wait()

    mate = partner[walk]
    own_count = counts[walk]
    arriving = jnp.maximum(counts[mate] - LIVE, 0)
    distance = jnp.bitwise_xor(mate, walk)

    def arrived(offset, size):
        value = moved_in[0, pl.ds(offset, size)].astype(jnp.float32)
        for bit in range(1, bit_count):
            other = moved_in[bit, pl.ds(offset, size)].astype(jnp.float32)
            value = pick(distance == 1 << bit, other, value)
        return value

    came_rows = [arrived(move * (own_rows + TAIL), own_rows) for move in range(MOVE)]
    came_logs = [split_log(arrived(move * (own_rows + TAIL) + own_rows, TAIL)) for move in range(MOVE)]
    for slot in range(LIVE):
        result, weight = jnp.zeros((own_rows, occ), jnp.float32), jnp.zeros((LOG_ROWS, occ), jnp.float32)
        for move in range(MOVE):
            flag = (slot - own_count == move) & (move < arriving)
            result = pick(flag, came_rows[move], result)
            weight = pick(flag, came_logs[move], weight)
        flag = slot < jnp.minimum(own_count, LIVE)
        new_out[slot] = pick(flag, mine[slot], result).astype(jnp.bfloat16)
        weight = pick(flag, logs[slot], weight)
        log_out[slot] = weight[0, 0]


def shards(walkers, inv_intersection, fields, cholesky, trial_rows, counts, partner):
    chol_count = lax.axis_size("chol")
    bit_count = lax.axis_size("walk").bit_length() - 1
    slots, depth, occ = walkers.shape
    vectors, rows, orbitals = cholesky.shape
    own_rows = rows // chol_count
    half = chol_count // 2
    others = half - 1
    bf16, f32 = jnp.bfloat16, jnp.float32
    dma = pltpu.SemaphoreType.DMA
    anywhere = pl.BlockSpec(memory_space=pl.ANY)
    vmem = pl.BlockSpec(memory_space=pltpu.VMEM)
    smem = pl.BlockSpec(memory_space=pltpu.SMEM)
    return pl.pallas_call(
        functools.partial(kernel, chol_count, bit_count),
        out_shape=(
            jax.ShapeDtypeStruct((LIVE, own_rows, occ), bf16),
            jax.ShapeDtypeStruct((LIVE,), f32),
        ),
        in_specs=[anywhere, anywhere, vmem, anywhere, anywhere, smem, smem],
        out_specs=(vmem, smem),
        scratch_shapes=[
            pltpu.VMEM((slots, chol_count, depth, occ), bf16),
            pltpu.VMEM((vectors, rows, orbitals), bf16),
            pltpu.VMEM((slots, occ, occ), bf16),
            pltpu.VMEM((rows, occ), bf16),
            pltpu.VMEM((slots, vectors * rows, occ), f32),
            pltpu.VMEM((slots, rows, occ), f32),
            pltpu.VMEM((slots, chol_count, own_rows, occ), f32),
            pltpu.VMEM((slots, LOG_ROWS, occ), f32),
            pltpu.VMEM((slots, own_rows, occ), f32),
            pltpu.VMEM((slots, half * own_rows + LOG_ROWS, occ), f32),
            pltpu.VMEM((slots, half * own_rows + LOG_ROWS, occ), f32),
            pltpu.VMEM((slots, others, own_rows + TAIL, occ), bf16),
            pltpu.VMEM((slots, others, own_rows + TAIL, occ), bf16),
            pltpu.VMEM((MOVE * (own_rows + TAIL), occ), bf16),
            pltpu.VMEM((bit_count, MOVE * (own_rows + TAIL), occ), bf16),
            dma((4,)),
            dma((2,)),
            dma((slots, others)),
            dma((slots, others)),
            dma((slots, others)),
            dma((slots, others)),
            dma((slots,)),
            dma((slots,)),
            dma((slots, others)),
            dma((slots, others)),
            dma((bit_count,)),
            dma((bit_count,)),
        ],
        compiler_params=pltpu.CompilerParams(
            collective_id=0, has_side_effects=True, vmem_limit_bytes=60 << 20
        ),
        cost_estimate=pl.CostEstimate(
            flops=2 * slots * vectors * rows * orbitals * occ,
            bytes_accessed=2 * (walkers.size + cholesky.size),
            transcendentals=0,
        ),
    )(walkers, inv_intersection, fields.T, cholesky, trial_rows, counts, partner)


def solution(mesh):
    in_specs = (
        P("walk", "chol", None),
        P("walk", None, None),
        P("walk", "chol"),
        P("chol", None, None),
        P(),
        P(),
        P(),
    )
    out_specs = (P("walk", "chol", None), P("walk"))
    return jax.shard_map(shards, mesh=mesh, in_specs=in_specs, out_specs=out_specs, check_vma=False)
```

```python
import functools

import jax
import jax.numpy as jnp
from jax import lax
from jax.experimental import pallas as pl
from jax.experimental.pallas import tpu as pltpu
from jax.sharding import PartitionSpec as P

LIVE = 4
MOVE = 2
PIECES = (1, 1, 1, 2)
VMEM_BYTES = 60 << 20
STEP_ROOT = 0.1
LOG_ROWS = 8
TAIL = 2 * LOG_ROWS
MESH = pl.DeviceIdType.MESH


def pick(flag, chosen, other):
    mask = jnp.broadcast_to(flag.astype(jnp.int32), chosen.shape) > 0
    return jnp.where(mask, chosen, other)


def kernel(
    chol_count,
    bit_count,
    walkers,
    minv_in,
    fields,
    chol_in,
    trial_in,
    counts,
    partner,
    new_out,
    log_out,
    phi,
    kept,
    came,
    chol,
    minv,
    came_minv,
    field_out,
    came_field,
    trial,
    prod,
    weighted,
    terms,
    logs,
    mine,
    sib_out,
    sib_in,
    far_out,
    far_in,
    load_sem,
    came_send,
    came_recv,
    minv_send,
    minv_recv,
    field_send,
    field_recv,
    near_send,
    near_recv,
    ahead_send,
    ahead_recv,
    pass_send,
    pass_recv,
    sib_send,
    sib_recv,
    far_send,
    far_recv,
):
    slots, depth, occ = walkers.shape
    vectors, rows, _ = chol_in.shape
    own_rows = rows // chol_count
    half = chol_count // 2
    walk = lax.axis_index("walk")
    me = lax.axis_index("chol")
    high, low = me // 2, me % 2
    sibling = 2 * high + 1 - low
    far_ids = [2 * lax.rem(high + step, half) + low for step in range(1, half)]
    from_high = [lax.rem(high - step + half, half) for step in range(1, half)]
    mates = [jnp.bitwise_xor(walk, 1 << bit) for bit in range(bit_count)]
    staying = LIVE - MOVE

    loads = [
        pltpu.make_async_copy(walkers.at[pl.ds(0, staying)], phi.at[pl.ds(0, staying), me], load_sem.at[0]),
        pltpu.make_async_copy(chol_in, chol, load_sem.at[1]),
        pltpu.make_async_copy(minv_in, minv, load_sem.at[2]),
        pltpu.make_async_copy(trial_in, trial, load_sem.at[3]),
        pltpu.make_async_copy(walkers.at[pl.ds(staying, MOVE)], kept, load_sem.at[4]),
    ]
    for load in loads:
        load.start()

    barrier = pltpu.get_barrier_semaphore()
    peers = [{"chol": sibling}] + [{"chol": far} for far in far_ids] + [{"walk": mate} for mate in mates]
    for peer in peers:
        pl.semaphore_signal(barrier, inc=1, device_id=peer, device_id_type=MESH)

    field_wide = fields[...].astype(jnp.float32)
    line = lax.broadcasted_iota(jnp.int32, field_out.shape, 0)
    spread = jnp.zeros(field_out.shape, jnp.float32)
    for move in range(MOVE):
        for vector in range(vectors):
            value = field_wide[vector : vector + 1, LIVE + move : LIVE + move + 1]
            spread = jnp.where(line == move * vectors + vector, value, spread)
    field_out[...] = spread.astype(jnp.bfloat16)

    pl.semaphore_wait(barrier, len(peers))

    def remote(src, dst, send, recv, peer):
        return pltpu.make_async_remote_copy(
            src_ref=src, dst_ref=dst, send_sem=send, recv_sem=recv, device_id=peer, device_id_type=MESH
        )

    def pieces(slot):
        count = PIECES[slot]
        return [(piece, pl.ds(piece * (depth // count), depth // count)) for piece in range(count)]

    sent = []

    def begin(copies):
        for copy in copies:
            copy.start()
        sent.extend(copies)
        return copies

    def send_ahead(slot, piece, span, source):
        return begin(
            [
                remote(
                    source,
                    phi.at[slot, me, span],
                    ahead_send.at[slot, step, piece],
                    ahead_recv.at[slot, step, piece],
                    {"chol": far_ids[step]},
                )
                for step in range(half - 1)
            ]
        )

    def send_near(slot, piece, span, source):
        return begin(
            [
                remote(
                    source,
                    phi.at[slot, me, span],
                    near_send.at[slot, piece],
                    near_recv.at[slot, piece],
                    {"chol": sibling},
                )
            ]
        )

    ahead, near, moved = {}, {}, {}

    def send_moved(move):
        for piece, span in pieces(staying + move):
            for bit in reversed(range(bit_count)):
                moved[move, piece, bit] = begin(
                    [
                        remote(
                            walkers.at[LIVE + move, span],
                            came.at[bit, move, span],
                            came_send.at[bit, move, piece],
                            came_recv.at[bit, move, piece],
                            {"walk": mates[bit]},
                        )
                    ]
                )[0]

    def send_own(slot):
        for piece, span in pieces(slot):
            ahead[slot, piece] = send_ahead(slot, piece, span, walkers.at[slot, span])
            near[slot, piece] = send_near(slot, piece, span, walkers.at[slot, span])

    send_own(0)
    send_moved(0)
    for slot in range(1, staying):
        send_own(slot)
    for move in range(1, MOVE):
        send_moved(move)
    small = []
    for bit in range(bit_count):
        small += begin(
            [
                remote(
                    minv_in.at[pl.ds(LIVE, MOVE)],
                    came_minv.at[bit],
                    minv_send.at[bit],
                    minv_recv.at[bit],
                    {"walk": mates[bit]},
                ),
                remote(
                    field_out, came_field.at[bit], field_send.at[bit], field_recv.at[bit], {"walk": mates[bit]}
                ),
            ]
        )

    mate = partner[walk]
    own_count = counts[walk]
    arriving = jnp.maximum(counts[mate] - LIVE, 0)
    distance = jnp.bitwise_xor(mate, walk)

    def arrived(read):
        value = read(0)
        for bit in range(1, bit_count):
            value = pick(distance == 1 << bit, read(bit), value)
        return value

    def place(move, read_came, read_own):
        value = read_own(move)
        for earlier in range(move):
            value = pick(own_count == LIVE - move + earlier, read_own(earlier), value)
        return pick(own_count < LIVE - move, arrived(lambda bit: read_came(bit, move)), value)

    def chol_half(index):
        columns = pl.ds(pl.multiple_of(index * 2 * depth, 2 * depth), 2 * depth)
        return chol[:, :, columns].reshape(vectors * rows, 2 * depth)

    def phi_half(slot, index):
        return phi[slot, pl.ds(2 * index, 2)].reshape(2 * depth, occ)

    def weigh(slot, inverse):
        weighted[slot] = lax.dot_general(
            trial[...], inverse, (((1,), (1,)), ((), ())), preferred_element_type=jnp.float32
        )

    def own_half(first):
        both = jnp.concatenate([phi_half(first, high), phi_half(first + 1, high)], axis=1)
        result = jnp.dot(chol_half(high), both, preferred_element_type=jnp.float32)
        prod[first] = result[:, :occ]
        prod[first + 1] = result[:, occ:]

    def forward(slot):
        passed = []
        for piece, span in pieces(slot):
            for step in range(half - 1):
                ahead[slot, piece][step].wait_recv()
                block = phi.at[slot, 2 * from_high[step] + low, span]
                passed += begin(
                    [
                        remote(
                            block,
                            block,
                            pass_send.at[slot, step, piece],
                            pass_recv.at[slot, step, piece],
                            {"chol": sibling},
                        )
                    ]
                )
        return passed

    def multiply(slot, passed, fields_of):
        for copy in passed:
            copy.wait_recv()
        total = prod[slot]
        for step in range(half - 1):
            total += jnp.dot(
                chol_half(from_high[step]),
                phi_half(slot, from_high[step]),
                preferred_element_type=jnp.float32,
            )
        total = total.reshape(vectors, rows, occ)
        increment = jnp.zeros((rows, occ), jnp.float32)
        weight = jnp.zeros((1, 1), jnp.float32)
        for vector in range(vectors):
            force_bias = -STEP_ROOT * jnp.sum(total[vector] * weighted[slot], keepdims=True)
            field = fields_of(vector)
            increment += (STEP_ROOT * (field - force_bias)) * total[vector]
            weight += field * force_bias - 0.5 * force_bias * force_bias
        terms[slot] = increment.reshape(chol_count, own_rows, occ)
        logs[slot] = jnp.broadcast_to(weight, (LOG_ROWS, occ))
        for index in range(half):
            sib_out[slot, pl.ds(index * own_rows, own_rows)] = terms[slot, 2 * index + 1 - low]
        sib_out[slot, pl.ds(half * own_rows, LOG_ROWS)] = logs[slot]
        return begin(
            [remote(sib_out.at[slot], sib_in.at[slot], sib_send.at[slot], sib_recv.at[slot], {"chol": sibling})]
        )[0]

    def chip_sum(slot, index):
        start = pl.multiple_of(index * own_rows, own_rows)
        return terms[slot, 2 * index + low] + sib_in[slot, pl.ds(start, own_rows)]

    def add_chip(slot, copy):
        copy.wait_recv()
        weight = logs[slot] + sib_in[slot, pl.ds(half * own_rows, LOG_ROWS)]
        logs[slot] = weight
        coarse = weight.astype(jnp.bfloat16).astype(jnp.float32)
        tail = jnp.concatenate([coarse, weight - coarse], axis=0).astype(jnp.bfloat16)
        copies = []
        for step in range(half - 1):
            far_out[slot, step, pl.ds(0, own_rows)] = chip_sum(slot, lax.rem(high + step + 1, half)).astype(
                jnp.bfloat16
            )
            far_out[slot, step, pl.ds(own_rows, TAIL)] = tail
            copies += begin(
                [
                    remote(
                        far_out.at[slot, step],
                        far_in.at[slot, step],
                        far_send.at[slot, step],
                        far_recv.at[slot, step],
                        {"chol": far_ids[step]},
                    )
                ]
            )
        mine[slot] = chip_sum(slot, high) + phi[slot, me, pl.ds(0, own_rows)].astype(jnp.float32)
        return copies

    def finish(slot, copies):
        result, weight = mine[slot], logs[slot]
        for step in range(half - 1):
            copies[step].wait_recv()
            result += far_in[slot, step, pl.ds(0, own_rows)].astype(jnp.float32)
            tail = far_in[slot, step, pl.ds(own_rows, TAIL)].astype(jnp.float32)
            weight += tail[:LOG_ROWS] + tail[LOG_ROWS:]
        return result, weight

    def place_walker(move):
        slot = staying + move
        for piece, span in pieces(slot):
            for bit in range(bit_count):
                moved[move, piece, bit].wait_recv()
            phi[slot, me, span] = place(
                move, lambda bit, move: came[bit, move, span], lambda own: kept[own, span]
            )
            source = phi.at[slot, me, span]
            ahead[slot, piece] = send_ahead(slot, piece, span, source)
            near[slot, piece] = send_near(slot, piece, span, source)

    def wait_near(slot):
        for piece, _ in pieces(slot):
            near[slot, piece][0].wait_recv()

    def own_field(slot):
        return lambda vector: field_wide[vector : vector + 1, slot : slot + 1]

    def placed_field(move):
        def of(vector):
            def read_came(bit, move):
                index = move * vectors + vector
                return came_field[bit].astype(jnp.float32)[index : index + 1, :1]

            return place(move, read_came, lambda own: own_field(staying + own)(vector))

        return of

    for load in loads[2:4]:
        load.wait()
    for slot in range(staying):
        weigh(slot, minv[slot])
    for load in loads[:2]:
        load.wait()
    for slot in range(staying):
        wait_near(slot)
    own_half(0)
    near_sum, far_sum = {}, {}
    passed = {0: forward(0)}
    near_sum[0] = multiply(0, passed[0], own_field(0))
    loads[4].wait()
    place_walker(0)
    passed[1] = forward(1)
    near_sum[1] = multiply(1, passed[1], own_field(1))
    far_sum[0] = add_chip(0, near_sum[0])
    place_walker(1)
    far_sum[1] = add_chip(1, near_sum[1])
    for copy in small:
        copy.wait_recv()
    for move in range(MOVE):
        weigh(
            staying + move,
            place(move, lambda bit, move: came_minv[bit, move], lambda own: minv[staying + own]),
        )
    wait_near(2)
    wait_near(3)
    own_half(2)
    passed[2] = forward(2)
    near_sum[2] = multiply(2, passed[2], placed_field(0))
    passed[3] = forward(3)
    far_sum[2] = add_chip(2, near_sum[2])
    near_sum[3] = multiply(3, passed[3], placed_field(1))
    done = [finish(slot, far_sum[slot]) for slot in range(2)]
    far_sum[3] = add_chip(3, near_sum[3])
    done += [finish(slot, far_sum[slot]) for slot in range(2, LIVE)]

    def balanced(index):
        first, second, third, fourth = [done[slot][index] for slot in range(LIVE)]
        return [
            first,
            pick(own_count == 1, third, second),
            pick((own_count == 2) | (own_count >= LIVE), third, fourth),
            pick(own_count == 3, third, fourth),
        ]

    new_rows, new_logs = balanced(0), balanced(1)
    for slot in range(LIVE):
        came_here = slot - own_count
        live = (slot < jnp.minimum(own_count, LIVE)) | ((came_here >= 0) & (came_here < arriving))
        new_out[slot] = pick(live, new_rows[slot], jnp.zeros_like(new_rows[slot])).astype(jnp.bfloat16)
        log_out[slot] = pick(live, new_logs[slot], jnp.zeros_like(new_logs[slot]))[0, 0]

    for copy in sent:
        copy.wait_send()


def shards(walkers, inv_intersection, fields, cholesky, trial_rows, counts, partner):
    chol_count = lax.axis_size("chol")
    bit_count = lax.axis_size("walk").bit_length() - 1
    slots, depth, occ = walkers.shape
    vectors, rows, orbitals = cholesky.shape
    own_rows = rows // chol_count
    half = chol_count // 2
    others = half - 1
    most = max(PIECES)
    field_rows = -(-MOVE * vectors // 16) * 16
    bf16, f32 = jnp.bfloat16, jnp.float32
    dma = pltpu.SemaphoreType.DMA
    anywhere = pl.BlockSpec(memory_space=pl.ANY)
    vmem = pl.BlockSpec(memory_space=pltpu.VMEM)
    smem = pl.BlockSpec(memory_space=pltpu.SMEM)
    return pl.pallas_call(
        functools.partial(kernel, chol_count, bit_count),
        out_shape=(
            jax.ShapeDtypeStruct((LIVE, own_rows, occ), bf16),
            jax.ShapeDtypeStruct((LIVE,), f32),
        ),
        in_specs=[anywhere, anywhere, vmem, anywhere, anywhere, smem, smem],
        out_specs=(vmem, smem),
        scratch_shapes=[
            pltpu.VMEM((LIVE, chol_count, depth, occ), bf16),
            pltpu.VMEM((MOVE, depth, occ), bf16),
            pltpu.VMEM((bit_count, MOVE, depth, occ), bf16),
            pltpu.VMEM((vectors, rows, orbitals), bf16),
            pltpu.VMEM((slots, occ, occ), bf16),
            pltpu.VMEM((bit_count, MOVE, occ, occ), bf16),
            pltpu.VMEM((field_rows, occ), bf16),
            pltpu.VMEM((bit_count, field_rows, occ), bf16),
            pltpu.VMEM((rows, occ), bf16),
            pltpu.VMEM((LIVE, vectors * rows, occ), f32),
            pltpu.VMEM((LIVE, rows, occ), f32),
            pltpu.VMEM((LIVE, chol_count, own_rows, occ), f32),
            pltpu.VMEM((LIVE, LOG_ROWS, occ), f32),
            pltpu.VMEM((LIVE, own_rows, occ), f32),
            pltpu.VMEM((LIVE, half * own_rows + LOG_ROWS, occ), f32),
            pltpu.VMEM((LIVE, half * own_rows + LOG_ROWS, occ), f32),
            pltpu.VMEM((LIVE, others, own_rows + TAIL, occ), bf16),
            pltpu.VMEM((LIVE, others, own_rows + TAIL, occ), bf16),
            dma((5,)),
            dma((bit_count, MOVE, most)),
            dma((bit_count, MOVE, most)),
            dma((bit_count,)),
            dma((bit_count,)),
            dma((bit_count,)),
            dma((bit_count,)),
            dma((LIVE, most)),
            dma((LIVE, most)),
            dma((LIVE, others, most)),
            dma((LIVE, others, most)),
            dma((LIVE, others, most)),
            dma((LIVE, others, most)),
            dma((LIVE,)),
            dma((LIVE,)),
            dma((LIVE, others)),
            dma((LIVE, others)),
        ],
        compiler_params=pltpu.CompilerParams(
            collective_id=0, has_side_effects=True, vmem_limit_bytes=VMEM_BYTES
        ),
        cost_estimate=pl.CostEstimate(
            flops=2 * LIVE * vectors * rows * orbitals * occ,
            bytes_accessed=2 * (walkers.size + cholesky.size),
            transcendentals=0,
        ),
    )(walkers, inv_intersection, fields.T, cholesky, trial_rows, counts, partner)


def solution(mesh):
    in_specs = (
        P("walk", "chol", None),
        P("walk", None, None),
        P("walk", "chol"),
        P("chol", None, None),
        P(),
        P(),
        P(),
    )
    out_specs = (P("walk", "chol", None), P("walk"))
    return jax.shard_map(shards, mesh=mesh, in_specs=in_specs, out_specs=out_specs, check_vma=False)
```

```python
import functools

import jax
import jax.numpy as jnp
from jax import lax
from jax.experimental import pallas as pl
from jax.experimental.pallas import tpu as pltpu
from jax.sharding import PartitionSpec as P

LIVE = 4
MOVE = 2
DEPTH = 2
VMEM_BYTES = 40 << 20
STEP_ROOT = 0.1
LOG_ROWS = 8
TAIL = 2 * LOG_ROWS
MESH = pl.DeviceIdType.MESH


def pick(flag, chosen, other):
    mask = jnp.broadcast_to(flag.astype(jnp.int32), chosen.shape) > 0
    return jnp.where(mask, chosen, other)


def kernel(
    chol_count,
    bit_count,
    walkers,
    minv_in,
    fields,
    chol_in,
    trial_in,
    counts,
    partner,
    new_out,
    log_out,
    phi,
    window,
    chol,
    minv,
    field_all,
    trial,
    prod,
    terms,
    base,
    sib_out,
    far_out,
    far_in,
    done,
    done_logs,
    moved_out,
    moved_in,
    load_sem,
    swap_send,
    swap_recv,
    near_send,
    near_recv,
    ahead_send,
    ahead_recv,
    sib_send,
    sib_recv,
    far_send,
    far_recv,
    moved_send,
    moved_recv,
):
    slots, depth, occ = walkers.shape
    vectors, rows, _ = chol_in.shape
    own_rows = rows // chol_count
    half = chol_count // 2
    pairs = slots // 2
    walk = lax.axis_index("walk")
    me = lax.axis_index("chol")
    high, low = me // 2, me % 2
    sibling = 2 * high + 1 - low
    to_high = [lax.rem(high + step, half) for step in range(1, half)]
    from_high = [lax.rem(high - step + half, half) for step in range(1, half)]
    mates = [jnp.bitwise_xor(walk, 1 << bit) for bit in range(bit_count)]
    fars = [(step, core) for step in range(half - 1) for core in range(2)]

    loads = [
        pltpu.make_async_copy(chol_in, chol.at[pl.ds(low * vectors, vectors)], load_sem.at[0]),
        pltpu.make_async_copy(minv_in, minv, load_sem.at[1]),
        pltpu.make_async_copy(trial_in, trial, load_sem.at[2]),
        pltpu.make_async_copy(walkers.at[:, pl.ds(0, own_rows)], window, load_sem.at[3]),
    ]
    own_loads = [
        pltpu.make_async_copy(walkers.at[2 * pair + low], phi.at[pair, me], load_sem.at[4 + pair])
        for pair in range(pairs)
    ]
    for load in loads + own_loads:
        load.start()

    barrier = pltpu.get_barrier_semaphore()
    peers = [{"chol": sibling}] + [{"chol": 2 * to_high[step] + core} for step, core in fars]
    peers += [{"walk": mate} for mate in mates]
    for peer in peers:
        pl.semaphore_signal(barrier, inc=1, device_id=peer, device_id_type=MESH)

    field_wide = fields[...].astype(jnp.float32)
    line = lax.broadcasted_iota(jnp.int32, field_all.shape[1:], 0)
    spread = jnp.zeros(field_all.shape[1:], jnp.float32)
    for slot in range(slots):
        for vector in range(vectors):
            value = field_wide[vector : vector + 1, slot : slot + 1]
            spread = jnp.where(line == slot * vectors + vector, value, spread)
    field_all[low] = spread.astype(jnp.bfloat16)

    pl.semaphore_wait(barrier, len(peers))

    def remote(src, dst, send, recv, peer):
        return pltpu.make_async_remote_copy(
            src_ref=src, dst_ref=dst, send_sem=send, recv_sem=recv, device_id=peer, device_id_type=MESH
        )

    sent = []

    def begin(copy):
        copy.start()
        sent.append(copy)
        return copy

    def send_ahead(pair):
        for step, core in fars:
            begin(
                remote(
                    walkers.at[2 * pair + core],
                    phi.at[pair, me],
                    ahead_send.at[pair, step, core],
                    ahead_recv.at[pair, step, low],
                    {"chol": 2 * to_high[step] + core},
                )
            )

    def wait_ahead(pair):
        for step, core in fars:
            remote(
                walkers.at[0],
                phi.at[pair, 2 * from_high[step] + core],
                ahead_send.at[pair, step, core],
                ahead_recv.at[pair, step, core],
                {"chol": sibling},
            ).wait_recv()

    order = list(range(LIVE // 2, pairs)) + list(range(LIVE // 2))
    for pair in order[:DEPTH]:
        send_ahead(pair)
    own_chol = pl.ds(low * vectors, vectors)
    swaps = [
        begin(remote(field_all.at[low], field_all.at[low], swap_send.at[0], swap_recv.at[0], {"chol": sibling})),
        begin(remote(chol_in, chol.at[own_chol], swap_send.at[1], swap_recv.at[1], {"chol": sibling})),
    ]
    near = [
        begin(
            remote(
                walkers.at[2 * pair + 1 - low],
                phi.at[pair, me],
                near_send.at[pair],
                near_recv.at[pair],
                {"chol": sibling},
            )
        )
        for pair in range(pairs)
    ]

    def chol_half(index):
        columns = pl.ds(pl.multiple_of(index * 2 * depth, 2 * depth), 2 * depth)
        return chol[:, :, columns].reshape(2 * vectors * rows, 2 * depth)

    def phi_half(pair, index):
        return phi[pair, pl.ds(2 * index, 2)].reshape(2 * depth, occ)

    for load in loads + own_loads:
        load.wait()
    for copy in near + swaps:
        copy.wait_recv()
    every = jnp.concatenate([phi_half(pair, high) for pair in range(pairs)], axis=1)
    result = jnp.dot(chol_half(high), every, preferred_element_type=jnp.float32)
    for pair in range(pairs):
        prod[pair] = result[:, pair * occ : (pair + 1) * occ]

    def multiply(pair):
        weighted = lax.dot_general(
            trial[...], minv[2 * pair + low], (((1,), (1,)), ((), ())), preferred_element_type=jnp.float32
        )
        wait_ahead(pair)
        later = order.index(pair) + DEPTH
        if later < pairs:
            send_ahead(order[later])
        total = prod[pair]
        for step in range(half - 1):
            total += jnp.dot(
                chol_half(from_high[step]),
                phi_half(pair, from_high[step]),
                preferred_element_type=jnp.float32,
            )
        total = total.reshape(2 * vectors, rows, occ)
        increment = jnp.zeros((rows, occ), jnp.float32)
        weight = jnp.zeros((1, 1), jnp.float32)
        for vector in range(2 * vectors):
            force_bias = -STEP_ROOT * jnp.sum(total[vector] * weighted, keepdims=True)
            values = field_all[vector // vectors].astype(jnp.float32)
            first = 2 * pair * vectors + vector % vectors
            field = pick(
                low == 0, values[first : first + 1, :1], values[first + vectors : first + vectors + 1, :1]
            )
            increment += (STEP_ROOT * (field - force_bias)) * total[vector]
            weight += field * force_bias - 0.5 * force_bias * force_bias
        terms[pair] = increment.reshape(chol_count, own_rows, occ)
        weight = jnp.broadcast_to(weight, (LOG_ROWS, occ))
        tail = split(weight)
        for step, core in fars:
            target = 2 * to_high[step] + core
            far_out[pair, step, core, pl.ds(0, own_rows)] = terms[pair, target].astype(jnp.bfloat16)
            far_out[pair, step, core, pl.ds(own_rows, TAIL)] = tail
            begin(
                remote(
                    far_out.at[pair, step, core],
                    far_in.at[pair, step, low],
                    far_send.at[pair, step, core],
                    far_recv.at[pair, step, low],
                    {"chol": target},
                )
            )
        sib_out[pair, pl.ds(0, own_rows)] = terms[pair, sibling]
        sib_out[pair, pl.ds(own_rows, LOG_ROWS)] = weight
        base[pair, low, pl.ds(0, own_rows)] = terms[pair, me]
        base[pair, low, pl.ds(own_rows, LOG_ROWS)] = weight
        begin(
            remote(
                sib_out.at[pair], base.at[pair, low], sib_send.at[pair], sib_recv.at[pair], {"chol": sibling}
            )
        )

    def split(weight):
        coarse = weight.astype(jnp.bfloat16).astype(jnp.float32)
        return jnp.concatenate([coarse, weight - coarse], axis=0).astype(jnp.bfloat16)

    def joined(tail):
        return tail[:LOG_ROWS] + tail[LOG_ROWS:]

    moved = [
        remote(moved_out, moved_in.at[bit], moved_send.at[bit], moved_recv.at[bit], {"walk": mates[bit]})
        for bit in range(bit_count)
    ]

    def finish(pair):
        remote(
            sib_out.at[pair], base.at[pair, 1 - low], sib_send.at[pair], sib_recv.at[pair], {"chol": sibling}
        ).wait_recv()
        for step, core in fars:
            remote(
                far_out.at[pair, step, core],
                far_in.at[pair, step, core],
                far_send.at[pair, step, core],
                far_recv.at[pair, step, core],
                {"chol": sibling},
            ).wait_recv()
        for core in range(2):
            slot = 2 * pair + core
            result = window[slot].astype(jnp.float32) + base[pair, core, pl.ds(0, own_rows)]
            weight = base[pair, core, pl.ds(own_rows, LOG_ROWS)]
            for step in range(half - 1):
                result += far_in[pair, step, core, pl.ds(0, own_rows)].astype(jnp.float32)
                weight += joined(far_in[pair, step, core, pl.ds(own_rows, TAIL)].astype(jnp.float32))
            if slot < LIVE:
                done[slot] = result
                done_logs[slot] = weight
            else:
                start = (slot - LIVE) * (own_rows + TAIL)
                moved_out[pl.ds(start, own_rows)] = result.astype(jnp.bfloat16)
                moved_out[pl.ds(start + own_rows, TAIL)] = split(weight)
        if pair == pairs - 1:
            for copy in moved:
                begin(copy)

    for position, pair in enumerate(order):
        multiply(pair)
        if position == 1:
            finish(order[0])
    for pair in order[1:]:
        finish(pair)

    mate = partner[walk]
    own_count = counts[walk]
    arriving = jnp.maximum(counts[mate] - LIVE, 0)
    distance = jnp.bitwise_xor(mate, walk)
    for copy in moved:
        copy.wait_recv()

    def arrived(offset, size):
        value = moved_in[0, pl.ds(offset, size)].astype(jnp.float32)
        for bit in range(1, bit_count):
            other = moved_in[bit, pl.ds(offset, size)].astype(jnp.float32)
            value = pick(distance == 1 << bit, other, value)
        return value

    came_rows = [arrived(move * (own_rows + TAIL), own_rows) for move in range(MOVE)]
    came_logs = [joined(arrived(move * (own_rows + TAIL) + own_rows, TAIL)) for move in range(MOVE)]
    for slot in range(LIVE):
        result, weight = jnp.zeros((own_rows, occ), jnp.float32), jnp.zeros((LOG_ROWS, occ), jnp.float32)
        for move in range(MOVE):
            flag = (slot - own_count == move) & (move < arriving)
            result = pick(flag, came_rows[move], result)
            weight = pick(flag, came_logs[move], weight)
        flag = slot < jnp.minimum(own_count, LIVE)
        new_out[slot] = pick(flag, done[slot], result).astype(jnp.bfloat16)
        weight = pick(flag, done_logs[slot], weight)
        log_out[slot] = weight[0, 0]

    for copy in sent:
        copy.wait_send()


def shards(walkers, inv_intersection, fields, cholesky, trial_rows, counts, partner):
    chol_count = lax.axis_size("chol")
    bit_count = lax.axis_size("walk").bit_length() - 1
    slots, depth, occ = walkers.shape
    vectors, rows, orbitals = cholesky.shape
    own_rows = rows // chol_count
    others = chol_count // 2 - 1
    pairs = slots // 2
    field_rows = -(-slots * vectors // 16) * 16
    bf16, f32 = jnp.bfloat16, jnp.float32
    dma = pltpu.SemaphoreType.DMA
    anywhere = pl.BlockSpec(memory_space=pl.ANY)
    vmem = pl.BlockSpec(memory_space=pltpu.VMEM)
    smem = pl.BlockSpec(memory_space=pltpu.SMEM)
    operands = (walkers, inv_intersection, fields.T, cholesky, trial_rows, counts, partner)
    operands = [pltpu.with_memory_space_constraint(operand, pltpu.HBM) for operand in operands]
    return pl.pallas_call(
        functools.partial(kernel, chol_count, bit_count),
        out_shape=(
            jax.ShapeDtypeStruct((LIVE, own_rows, occ), bf16),
            jax.ShapeDtypeStruct((LIVE,), f32),
        ),
        in_specs=[anywhere, anywhere, vmem, anywhere, anywhere, smem, smem],
        out_specs=(vmem, smem),
        scratch_shapes=[
            pltpu.VMEM((pairs, chol_count, depth, occ), bf16),
            pltpu.VMEM((slots, own_rows, occ), bf16),
            pltpu.VMEM((2 * vectors, rows, orbitals), bf16),
            pltpu.VMEM((slots, occ, occ), bf16),
            pltpu.VMEM((2, field_rows, occ), bf16),
            pltpu.VMEM((rows, occ), bf16),
            pltpu.VMEM((pairs, 2 * vectors * rows, occ), f32),
            pltpu.VMEM((pairs, chol_count, own_rows, occ), f32),
            pltpu.VMEM((pairs, 2, own_rows + LOG_ROWS, occ), f32),
            pltpu.VMEM((pairs, own_rows + LOG_ROWS, occ), f32),
            pltpu.VMEM((pairs, others, 2, own_rows + TAIL, occ), bf16),
            pltpu.VMEM((pairs, others, 2, own_rows + TAIL, occ), bf16),
            pltpu.VMEM((LIVE, own_rows, occ), f32),
            pltpu.VMEM((LIVE, LOG_ROWS, occ), f32),
            pltpu.VMEM((MOVE * (own_rows + TAIL), occ), bf16),
            pltpu.VMEM((bit_count, MOVE * (own_rows + TAIL), occ), bf16),
            dma((4 + pairs,)),
            dma((2,)),
            dma((2,)),
            dma((pairs,)),
            dma((pairs,)),
            dma((pairs, others, 2)),
            dma((pairs, others, 2)),
            dma((pairs,)),
            dma((pairs,)),
            dma((pairs, others, 2)),
            dma((pairs, others, 2)),
            dma((bit_count,)),
            dma((bit_count,)),
        ],
        compiler_params=pltpu.CompilerParams(
            collective_id=0, has_side_effects=True, vmem_limit_bytes=VMEM_BYTES
        ),
        cost_estimate=pl.CostEstimate(
            flops=2 * slots * vectors * rows * orbitals * occ,
            bytes_accessed=2 * (walkers.size + cholesky.size),
            transcendentals=0,
        ),
    )(*operands)


def solution(mesh):
    in_specs = (
        P("walk", "chol", None),
        P("walk", None, None),
        P("walk", "chol"),
        P("chol", None, None),
        P(),
        P(),
        P(),
    )
    out_specs = (P("walk", "chol", None), P("walk"))
    return jax.shard_map(shards, mesh=mesh, in_specs=in_specs, out_specs=out_specs, check_vma=False)
```

```python
import functools

import jax
import jax.numpy as jnp
from jax import lax
from jax.experimental import pallas as pl
from jax.experimental.pallas import tpu as pltpu
from jax.sharding import PartitionSpec as P

LIVE = 4
VMEM_BYTES = 40 << 20
STEP_ROOT = 0.1
LOG_ROWS = 8
TAIL = 2 * LOG_ROWS
MESH = pl.DeviceIdType.MESH


def pick(flag, chosen, other):
    mask = jnp.broadcast_to(flag.astype(jnp.int32), chosen.shape) > 0
    return jnp.where(mask, chosen, other)


def kernel(
    chol_count,
    bit_count,
    walkers,
    minv_in,
    fields,
    chol_in,
    trial_in,
    counts,
    partner,
    new_out,
    log_out,
    phi,
    window,
    kept,
    placed,
    came,
    chol,
    minv,
    came_minv,
    field_all,
    came_field,
    trial,
    prod,
    terms,
    base,
    sib_out,
    far_out,
    far_in,
    done,
    done_logs,
    moved_out,
    moved_in,
    load_sem,
    came_send,
    came_recv,
    swap_send,
    swap_recv,
    near_send,
    near_recv,
    ahead_send,
    ahead_recv,
    sib_send,
    sib_recv,
    far_send,
    far_recv,
    moved_send,
    moved_recv,
):
    slots, depth, occ = walkers.shape
    vectors, rows, _ = chol_in.shape
    own_rows = rows // chol_count
    half = chol_count // 2
    pairs = slots // 2
    walk = lax.axis_index("walk")
    me = lax.axis_index("chol")
    high, low = me // 2, me % 2
    sibling = 2 * high + 1 - low
    to_high = [lax.rem(high + step, half) for step in range(1, half)]
    from_high = [lax.rem(high - step + half, half) for step in range(1, half)]
    mates = [jnp.bitwise_xor(walk, 1 << bit) for bit in range(bit_count)]
    fars = [(step, core) for step in range(half - 1) for core in range(2)]

    loads = [
        pltpu.make_async_copy(chol_in, chol.at[pl.ds(low * vectors, vectors)], load_sem.at[0]),
        pltpu.make_async_copy(minv_in, minv, load_sem.at[1]),
        pltpu.make_async_copy(trial_in, trial, load_sem.at[2]),
        pltpu.make_async_copy(walkers.at[:, pl.ds(0, own_rows)], window, load_sem.at[3]),
        pltpu.make_async_copy(walkers.at[LIVE - 1], kept, load_sem.at[4 + pairs]),
    ]
    own_loads = [
        pltpu.make_async_copy(walkers.at[2 * pair + low], phi.at[pair, me], load_sem.at[4 + pair])
        for pair in range(pairs)
    ]
    for load in loads + own_loads:
        load.start()

    barrier = pltpu.get_barrier_semaphore()
    peers = [{"chol": sibling}] + [{"chol": 2 * to_high[step] + core} for step, core in fars]
    peers += [{"walk": mate} for mate in mates]
    for peer in peers:
        pl.semaphore_signal(barrier, inc=1, device_id=peer, device_id_type=MESH)

    field_wide = fields[...].astype(jnp.float32)
    line = lax.broadcasted_iota(jnp.int32, field_all.shape[1:], 0)
    spread = jnp.zeros(field_all.shape[1:], jnp.float32)
    for slot in range(slots):
        for vector in range(vectors):
            value = field_wide[vector : vector + 1, slot : slot + 1]
            spread = jnp.where(line == slot * vectors + vector, value, spread)
    field_all[low] = spread.astype(jnp.bfloat16)

    pl.semaphore_wait(barrier, len(peers))

    def remote(src, dst, send, recv, peer):
        return pltpu.make_async_remote_copy(
            src_ref=src, dst_ref=dst, send_sem=send, recv_sem=recv, device_id=peer, device_id_type=MESH
        )

    sent = []

    def begin(copy):
        copy.start()
        sent.append(copy)
        return copy

    def send_ahead(slot, source):
        for step in range(half - 1):
            begin(
                remote(
                    source,
                    phi.at[slot // 2, me],
                    ahead_send.at[slot // 2, step, slot % 2],
                    ahead_recv.at[slot // 2, step, low],
                    {"chol": 2 * to_high[step] + slot % 2},
                )
            )

    def wait_ahead(pair):
        for step, core in fars:
            remote(
                walkers.at[0],
                phi.at[pair, 2 * from_high[step] + core],
                ahead_send.at[pair, step, core],
                ahead_recv.at[pair, step, core],
                {"chol": sibling},
            ).wait_recv()

    def near_copy(pair, source):
        return remote(source, phi.at[pair, me], near_send.at[pair], near_recv.at[pair], {"chol": sibling})

    home, last = LIVE // 2, LIVE // 2 - 1
    send_ahead(LIVE, walkers.at[LIVE])
    moves = [
        begin(
            remote(
                walkers.at[LIVE + 1],
                came.at[bit],
                came_send.at[0, bit],
                came_recv.at[0, bit],
                {"walk": mates[bit]},
            )
        )
        for bit in reversed(range(bit_count))
    ]
    send_ahead(0, walkers.at[0])
    send_ahead(1, walkers.at[1])
    swaps = [
        begin(remote(field_all.at[low], field_all.at[low], swap_send.at[0], swap_recv.at[0], {"chol": sibling})),
        begin(
            remote(
                chol_in,
                chol.at[pl.ds(low * vectors, vectors)],
                swap_send.at[1],
                swap_recv.at[1],
                {"chol": sibling},
            )
        ),
    ]
    near = [near_copy(pair, walkers.at[2 * pair + 1 - low]) for pair in range(last)]
    for copy in near:
        begin(copy)

    @pl.when(low == 1)
    def _():
        near_copy(home, walkers.at[LIVE]).start()
        near_copy(last, walkers.at[LIVE - 2]).start()

    moves += [
        begin(
            remote(
                minv_in.at[LIVE + 1],
                came_minv.at[bit],
                came_send.at[1, bit],
                came_recv.at[1, bit],
                {"walk": mates[bit]},
            )
        )
        for bit in range(bit_count)
    ]
    swaps[0].wait_recv()
    moves += [
        begin(
            remote(
                field_all,
                came_field.at[bit],
                came_send.at[2, bit],
                came_recv.at[2, bit],
                {"walk": mates[bit]},
            )
        )
        for bit in range(bit_count)
    ]
    send_ahead(LIVE - 2, walkers.at[LIVE - 2])

    mate = partner[walk]
    own_count = counts[walk]
    arriving = jnp.maximum(counts[mate] - LIVE, 0)
    distance = jnp.bitwise_xor(mate, walk)

    def arrived(read):
        value = read(0)
        for bit in range(1, bit_count):
            value = pick(distance == 1 << bit, read(bit), value)
        return value

    def place(own, read):
        return pick(own_count < LIVE, arrived(read), own)

    def chol_half(index):
        columns = pl.ds(pl.multiple_of(index * 2 * depth, 2 * depth), 2 * depth)
        return chol[:, :, columns].reshape(2 * vectors * rows, 2 * depth)

    def phi_half(pair, index):
        return phi[pair, pl.ds(2 * index, 2)].reshape(2 * depth, occ)

    for load in loads + own_loads:
        load.wait()
    for copy in near + swaps[1:]:
        copy.wait_recv()

    @pl.when(low == 0)
    def _():
        near_copy(home, walkers.at[LIVE]).wait_recv()

    def own_half(some):
        every = jnp.concatenate([phi_half(pair, high) for pair in some], axis=1)
        result = jnp.dot(chol_half(high), every, preferred_element_type=jnp.float32)
        for index, pair in enumerate(some):
            prod[pair] = result[:, index * occ : (index + 1) * occ]

    own_half([home] + list(range(last)))

    def place_last():
        for copy in moves:
            copy.wait_recv()
        placed[...] = place(kept[...], lambda bit: came[bit])
        send_ahead(LIVE - 1, placed)

        @pl.when(low == 0)
        def _():
            near_copy(last, placed).start()

        phi[last, me] = pick(low == 1, placed[...], phi[last, me])

    def field_of(pair, vector):
        values = field_all[vector // vectors].astype(jnp.float32)
        place_in = vector % vectors

        def at(array, slot):
            line = slot * vectors + place_in
            return array[line : line + 1, :1]

        second = at(values, 2 * pair + 1)
        if pair == last:
            second = place(
                second, lambda bit: at(came_field[bit, vector // vectors].astype(jnp.float32), LIVE + 1)
            )
        return pick(low == 0, at(values, 2 * pair), second)

    def far_copy(pair, step, core):
        return remote(
            far_out.at[pair, step, core],
            far_in.at[pair, step, low],
            far_send.at[pair, step, core],
            far_recv.at[pair, step, low],
            {"chol": 2 * to_high[step] + core},
        )

    def sib_copy(pair):
        return remote(
            sib_out.at[pair], base.at[pair, low], sib_send.at[pair], sib_recv.at[pair], {"chol": sibling}
        )

    def multiply(pair):
        inverse = minv[2 * pair + low]
        if pair == last:
            inverse = pick(low == 0, inverse, place(minv[LIVE - 1], lambda bit: came_minv[bit]))
        weighted = lax.dot_general(
            trial[...], inverse, (((1,), (1,)), ((), ())), preferred_element_type=jnp.float32
        )
        wait_ahead(pair)
        total = prod[pair]
        for step in range(half - 1):
            total += jnp.dot(
                chol_half(from_high[step]),
                phi_half(pair, from_high[step]),
                preferred_element_type=jnp.float32,
            )
        total = total.reshape(2 * vectors, rows, occ)
        increment = jnp.zeros((rows, occ), jnp.float32)
        weight = jnp.zeros((1, 1), jnp.float32)
        for vector in range(2 * vectors):
            force_bias = -STEP_ROOT * jnp.sum(total[vector] * weighted, keepdims=True)
            field = field_of(pair, vector)
            increment += (STEP_ROOT * (field - force_bias)) * total[vector]
            weight += field * force_bias - 0.5 * force_bias * force_bias
        terms[pair] = increment.reshape(chol_count, own_rows, occ)
        weight = jnp.broadcast_to(weight, (LOG_ROWS, occ))
        tail = split(weight)
        for step, core in fars:
            target = 2 * to_high[step] + core
            far_out[pair, step, core, pl.ds(0, own_rows)] = terms[pair, target].astype(jnp.bfloat16)
            far_out[pair, step, core, pl.ds(own_rows, TAIL)] = tail
            far_copy(pair, step, core).start()
        sib_out[pair, pl.ds(0, own_rows)] = terms[pair, sibling]
        sib_out[pair, pl.ds(own_rows, LOG_ROWS)] = weight
        base[pair, low, pl.ds(0, own_rows)] = terms[pair, me]
        base[pair, low, pl.ds(own_rows, LOG_ROWS)] = weight
        sib_copy(pair).start()

    def split(weight):
        coarse = weight.astype(jnp.bfloat16).astype(jnp.float32)
        return jnp.concatenate([coarse, weight - coarse], axis=0).astype(jnp.bfloat16)

    def joined(tail):
        return tail[:LOG_ROWS] + tail[LOG_ROWS:]

    moved = [
        remote(moved_out, moved_in.at[bit], moved_send.at[bit], moved_recv.at[bit], {"walk": mates[bit]})
        for bit in range(bit_count)
    ]

    def finish(pair):
        cores = 1 if pair == home else 2

        def wait_sibling():
            remote(
                sib_out.at[pair],
                base.at[pair, 1 - low],
                sib_send.at[pair],
                sib_recv.at[pair],
                {"chol": sibling},
            ).wait_recv()

        if pair == home:
            pl.when(low == 1)(wait_sibling)
        else:
            wait_sibling()
        for step, core in fars:
            if core < cores:
                remote(
                    far_out.at[pair, step, core],
                    far_in.at[pair, step, core],
                    far_send.at[pair, step, core],
                    far_recv.at[pair, step, core],
                    {"chol": sibling},
                ).wait_recv()
        for core in range(cores):
            slot = 2 * pair + core
            rows_in = placed[pl.ds(0, own_rows)] if slot == LIVE - 1 else window[slot]
            result = rows_in.astype(jnp.float32) + base[pair, core, pl.ds(0, own_rows)]
            weight = base[pair, core, pl.ds(own_rows, LOG_ROWS)]
            for step in range(half - 1):
                result += far_in[pair, step, core, pl.ds(0, own_rows)].astype(jnp.float32)
                weight += joined(far_in[pair, step, core, pl.ds(own_rows, TAIL)].astype(jnp.float32))
            if slot < LIVE:
                done[slot] = result
                done_logs[slot] = weight
            else:
                moved_out[pl.ds(0, own_rows)] = result.astype(jnp.bfloat16)
                moved_out[pl.ds(own_rows, TAIL)] = split(weight)
        if pair == home:
            for copy in moved:
                begin(copy)

    pl.when(low == 0)(functools.partial(multiply, home))
    place_last()
    for pair in range(last):
        multiply(pair)
    finish(home)
    near_copy(last, placed).wait_recv()
    own_half([last])
    multiply(last)
    for pair in range(home):
        finish(pair)
    for copy in moved:
        copy.wait_recv()

    came_rows = arrived(lambda bit: moved_in[bit, pl.ds(0, own_rows)].astype(jnp.float32))
    came_logs = joined(arrived(lambda bit: moved_in[bit, pl.ds(own_rows, TAIL)].astype(jnp.float32)))

    def choose(slot, own, first, second):
        came_here = slot - own_count
        value = pick((came_here == 1) & (arriving > 1), second, jnp.zeros_like(own))
        value = pick((came_here == 0) & (arriving > 0), first, value)
        return pick(slot < jnp.minimum(own_count, LIVE), own, value)

    for slot in range(LIVE):
        new_out[slot] = choose(slot, done[slot], came_rows, done[LIVE - 1]).astype(jnp.bfloat16)
        log_out[slot] = choose(slot, done_logs[slot], came_logs, done_logs[LIVE - 1])[0, 0]

    for copy in sent:
        copy.wait_send()
    near_copy(last, placed).wait_send()
    for pair in range(home):
        sib_copy(pair).wait_send()
        for step, core in fars:
            far_copy(pair, step, core).wait_send()

    @pl.when(low == 0)
    def _():
        sib_copy(home).wait_send()
        for step, core in fars:
            far_copy(home, step, core).wait_send()

    @pl.when(low == 1)
    def _():
        near_copy(home, walkers.at[LIVE]).wait_send()


def shards(walkers, inv_intersection, fields, cholesky, trial_rows, counts, partner):
    chol_count = lax.axis_size("chol")
    bit_count = lax.axis_size("walk").bit_length() - 1
    slots, depth, occ = walkers.shape
    vectors, rows, orbitals = cholesky.shape
    own_rows = rows // chol_count
    others = chol_count // 2 - 1
    pairs = slots // 2
    field_rows = -(-slots * vectors // 16) * 16
    bf16, f32 = jnp.bfloat16, jnp.float32
    dma = pltpu.SemaphoreType.DMA
    anywhere = pl.BlockSpec(memory_space=pl.ANY)
    vmem = pl.BlockSpec(memory_space=pltpu.VMEM)
    smem = pl.BlockSpec(memory_space=pltpu.SMEM)
    operands = (walkers, inv_intersection, fields.T, cholesky, trial_rows, counts, partner)
    operands = [pltpu.with_memory_space_constraint(operand, pltpu.HBM) for operand in operands]
    return pl.pallas_call(
        functools.partial(kernel, chol_count, bit_count),
        out_shape=(
            jax.ShapeDtypeStruct((LIVE, own_rows, occ), bf16),
            jax.ShapeDtypeStruct((LIVE,), f32),
        ),
        in_specs=[anywhere, anywhere, vmem, anywhere, anywhere, smem, smem],
        out_specs=(vmem, smem),
        scratch_shapes=[
            pltpu.VMEM((pairs, chol_count, depth, occ), bf16),
            pltpu.VMEM((slots, own_rows, occ), bf16),
            pltpu.VMEM((depth, occ), bf16),
            pltpu.VMEM((depth, occ), bf16),
            pltpu.VMEM((bit_count, depth, occ), bf16),
            pltpu.VMEM((2 * vectors, rows, orbitals), bf16),
            pltpu.VMEM((slots, occ, occ), bf16),
            pltpu.VMEM((bit_count, occ, occ), bf16),
            pltpu.VMEM((2, field_rows, occ), bf16),
            pltpu.VMEM((bit_count, 2, field_rows, occ), bf16),
            pltpu.VMEM((rows, occ), bf16),
            pltpu.VMEM((pairs, 2 * vectors * rows, occ), f32),
            pltpu.VMEM((pairs, chol_count, own_rows, occ), f32),
            pltpu.VMEM((pairs, 2, own_rows + LOG_ROWS, occ), f32),
            pltpu.VMEM((pairs, own_rows + LOG_ROWS, occ), f32),
            pltpu.VMEM((pairs, others, 2, own_rows + TAIL, occ), bf16),
            pltpu.VMEM((pairs, others, 2, own_rows + TAIL, occ), bf16),
            pltpu.VMEM((LIVE, own_rows, occ), f32),
            pltpu.VMEM((LIVE, LOG_ROWS, occ), f32),
            pltpu.VMEM((own_rows + TAIL, occ), bf16),
            pltpu.VMEM((bit_count, own_rows + TAIL, occ), bf16),
            dma((5 + pairs,)),
            dma((3, bit_count)),
            dma((3, bit_count)),
            dma((2,)),
            dma((2,)),
            dma((pairs,)),
            dma((pairs,)),
            dma((pairs, others, 2)),
            dma((pairs, others, 2)),
            dma((pairs,)),
            dma((pairs,)),
            dma((pairs, others, 2)),
            dma((pairs, others, 2)),
            dma((bit_count,)),
            dma((bit_count,)),
        ],
        compiler_params=pltpu.CompilerParams(
            collective_id=0, has_side_effects=True, vmem_limit_bytes=VMEM_BYTES
        ),
        cost_estimate=pl.CostEstimate(
            flops=2 * slots * vectors * rows * orbitals * occ,
            bytes_accessed=2 * (walkers.size + cholesky.size),
            transcendentals=0,
        ),
    )(*operands)


def solution(mesh):
    in_specs = (
        P("walk", "chol", None),
        P("walk", None, None),
        P("walk", "chol"),
        P("chol", None, None),
        P(),
        P(),
        P(),
    )
    out_specs = (P("walk", "chol", None), P("walk"))
    return jax.shard_map(shards, mesh=mesh, in_specs=in_specs, out_specs=out_specs, check_vma=False)
```

```python
import functools

import jax
import jax.numpy as jnp
from jax import lax
from jax.experimental import pallas as pl
from jax.experimental.pallas import tpu as pltpu
from jax.sharding import PartitionSpec as P

LIVE = 4
VMEM_BYTES = 40 << 20
STEP_ROOT = 0.1
LOG_ROWS = 8
TAIL = 2 * LOG_ROWS
MESH = pl.DeviceIdType.MESH


def pick(flag, chosen, other):
    mask = jnp.broadcast_to(flag.astype(jnp.int32), chosen.shape) > 0
    return jnp.where(mask, chosen, other)


def kernel(
    chol_count,
    bit_count,
    walkers,
    minv_in,
    fields,
    chol_in,
    trial_in,
    counts_in,
    partner_in,
    new_out,
    log_out,
    counts,
    partner,
    phi,
    window,
    kept,
    placed,
    came,
    chol,
    minv,
    came_minv,
    field_all,
    came_field,
    trial,
    prod,
    terms,
    base,
    sib_out,
    far_out,
    far_in,
    done,
    done_logs,
    moved_out,
    moved_in,
    load_sem,
    came_send,
    came_recv,
    swap_send,
    swap_recv,
    near_send,
    near_recv,
    ahead_send,
    ahead_recv,
    sib_send,
    sib_recv,
    far_send,
    far_recv,
    moved_send,
    moved_recv,
):
    slots, depth, occ = walkers.shape
    vectors, rows, _ = chol_in.shape
    own_rows = rows // chol_count
    half = chol_count // 2
    pairs = slots // 2
    walk = lax.axis_index("walk")
    me = lax.axis_index("chol")
    high, low = me // 2, me % 2
    sibling = 2 * high + 1 - low
    to_high = [lax.rem(high + step, half) for step in range(1, half)]
    from_high = [lax.rem(high - step + half, half) for step in range(1, half)]
    mates = [jnp.bitwise_xor(walk, 1 << bit) for bit in range(bit_count)]
    fars = [(step, core) for step in range(half - 1) for core in range(2)]

    loads = [
        pltpu.make_async_copy(chol_in, chol.at[pl.ds(low * vectors, vectors)], load_sem.at[0]),
        pltpu.make_async_copy(minv_in, minv, load_sem.at[1]),
        pltpu.make_async_copy(trial_in, trial, load_sem.at[2]),
        pltpu.make_async_copy(walkers.at[:, pl.ds(0, own_rows)], window, load_sem.at[3]),
        pltpu.make_async_copy(walkers.at[LIVE - 1], kept, load_sem.at[4 + pairs]),
    ]
    table_loads = [
        pltpu.make_async_copy(counts_in, counts, load_sem.at[5 + pairs]),
        pltpu.make_async_copy(partner_in, partner, load_sem.at[6 + pairs]),
    ]
    own_loads = [
        pltpu.make_async_copy(walkers.at[2 * pair + low], phi.at[pair, me], load_sem.at[4 + pair])
        for pair in range(pairs)
    ]
    for load in loads + own_loads + table_loads:
        load.start()

    barrier = pltpu.get_barrier_semaphore()
    peers = [{"chol": sibling}] + [{"chol": 2 * to_high[step] + core} for step, core in fars]
    peers += [{"walk": mate} for mate in mates]
    for peer in peers:
        pl.semaphore_signal(barrier, inc=1, device_id=peer, device_id_type=MESH)

    field_wide = fields[...].astype(jnp.float32)
    line = lax.broadcasted_iota(jnp.int32, field_all.shape[1:], 0)
    spread = jnp.zeros(field_all.shape[1:], jnp.float32)
    for slot in range(slots):
        for vector in range(vectors):
            value = field_wide[vector : vector + 1, slot : slot + 1]
            spread = jnp.where(line == slot * vectors + vector, value, spread)
    field_all[low] = spread.astype(jnp.bfloat16)

    pl.semaphore_wait(barrier, len(peers))

    def remote(src, dst, send, recv, peer):
        return pltpu.make_async_remote_copy(
            src_ref=src, dst_ref=dst, send_sem=send, recv_sem=recv, device_id=peer, device_id_type=MESH
        )

    sent = []

    def begin(copy):
        copy.start()
        sent.append(copy)
        return copy

    def send_ahead(slot, source):
        for step in range(half - 1):
            begin(
                remote(
                    source,
                    phi.at[slot // 2, me],
                    ahead_send.at[slot // 2, step, slot % 2],
                    ahead_recv.at[slot // 2, step, low],
                    {"chol": 2 * to_high[step] + slot % 2},
                )
            )

    def wait_ahead(pair):
        for step, core in fars:
            remote(
                walkers.at[0],
                phi.at[pair, 2 * from_high[step] + core],
                ahead_send.at[pair, step, core],
                ahead_recv.at[pair, step, core],
                {"chol": sibling},
            ).wait_recv()

    def near_copy(pair, source):
        return remote(source, phi.at[pair, me], near_send.at[pair], near_recv.at[pair], {"chol": sibling})

    home, last = LIVE // 2, LIVE // 2 - 1
    send_ahead(LIVE, walkers.at[LIVE])
    moves = [
        begin(
            remote(
                walkers.at[LIVE + 1],
                came.at[bit],
                came_send.at[0, bit],
                came_recv.at[0, bit],
                {"walk": mates[bit]},
            )
        )
        for bit in reversed(range(bit_count))
    ]
    send_ahead(0, walkers.at[0])
    send_ahead(1, walkers.at[1])
    swaps = [
        begin(remote(field_all.at[low], field_all.at[low], swap_send.at[0], swap_recv.at[0], {"chol": sibling})),
        begin(
            remote(
                chol_in,
                chol.at[pl.ds(low * vectors, vectors)],
                swap_send.at[1],
                swap_recv.at[1],
                {"chol": sibling},
            )
        ),
    ]
    near = [near_copy(pair, walkers.at[2 * pair + 1 - low]) for pair in range(last)]
    for copy in near:
        begin(copy)

    @pl.when(low == 1)
    def _():
        near_copy(home, walkers.at[LIVE]).start()
        near_copy(last, walkers.at[LIVE - 2]).start()

    moves += [
        begin(
            remote(
                minv_in.at[LIVE + 1],
                came_minv.at[bit],
                came_send.at[1, bit],
                came_recv.at[1, bit],
                {"walk": mates[bit]},
            )
        )
        for bit in range(bit_count)
    ]
    swaps[0].wait_recv()
    moves += [
        begin(
            remote(
                field_all,
                came_field.at[bit],
                came_send.at[2, bit],
                came_recv.at[2, bit],
                {"walk": mates[bit]},
            )
        )
        for bit in range(bit_count)
    ]
    send_ahead(LIVE - 2, walkers.at[LIVE - 2])

    for load in table_loads:
        load.wait()
    mate = partner[walk]
    own_count = counts[walk]
    arriving = jnp.maximum(counts[mate] - LIVE, 0)
    distance = jnp.bitwise_xor(mate, walk)

    def arrived(read):
        value = read(0)
        for bit in range(1, bit_count):
            value = pick(distance == 1 << bit, read(bit), value)
        return value

    def place(own, read):
        return pick(own_count < LIVE, arrived(read), own)

    def chol_half(index):
        columns = pl.ds(pl.multiple_of(index * 2 * depth, 2 * depth), 2 * depth)
        return chol[:, :, columns].reshape(2 * vectors * rows, 2 * depth)

    def phi_half(pair, index):
        return phi[pair, pl.ds(2 * index, 2)].reshape(2 * depth, occ)

    for load in loads + own_loads:
        load.wait()
    for copy in near + swaps[1:]:
        copy.wait_recv()

    @pl.when(low == 0)
    def _():
        near_copy(home, walkers.at[LIVE]).wait_recv()

    def own_half(some):
        every = jnp.concatenate([phi_half(pair, high) for pair in some], axis=1)
        result = jnp.dot(chol_half(high), every, preferred_element_type=jnp.float32)
        for index, pair in enumerate(some):
            prod[pair] = result[:, index * occ : (index + 1) * occ]

    own_half([home] + list(range(last)))

    def place_last():
        for copy in moves:
            copy.wait_recv()
        placed[...] = place(kept[...], lambda bit: came[bit])
        send_ahead(LIVE - 1, placed)

        @pl.when(low == 0)
        def _():
            near_copy(last, placed).start()

        phi[last, me] = pick(low == 1, placed[...], phi[last, me])

    def field_of(pair, vector):
        values = field_all[vector // vectors].astype(jnp.float32)
        place_in = vector % vectors

        def at(array, slot):
            line = slot * vectors + place_in
            return array[line : line + 1, :1]

        second = at(values, 2 * pair + 1)
        if pair == last:
            second = place(
                second, lambda bit: at(came_field[bit, vector // vectors].astype(jnp.float32), LIVE + 1)
            )
        return pick(low == 0, at(values, 2 * pair), second)

    def far_copy(pair, step, core):
        return remote(
            far_out.at[pair, step, core],
            far_in.at[pair, step, low],
            far_send.at[pair, step, core],
            far_recv.at[pair, step, low],
            {"chol": 2 * to_high[step] + core},
        )

    def sib_copy(pair):
        return remote(
            sib_out.at[pair], base.at[pair, low], sib_send.at[pair], sib_recv.at[pair], {"chol": sibling}
        )

    def multiply(pair):
        inverse = minv[2 * pair + low]
        if pair == last:
            inverse = pick(low == 0, inverse, place(minv[LIVE - 1], lambda bit: came_minv[bit]))
        weighted = lax.dot_general(
            trial[...], inverse, (((1,), (1,)), ((), ())), preferred_element_type=jnp.float32
        )
        field_values = [field_of(pair, vector) for vector in range(2 * vectors)]
        wait_ahead(pair)
        total = prod[pair]
        for step in range(half - 1):
            total += jnp.dot(
                chol_half(from_high[step]),
                phi_half(pair, from_high[step]),
                preferred_element_type=jnp.float32,
            )
        total = total.reshape(2 * vectors, rows, occ)
        increment = jnp.zeros((rows, occ), jnp.float32)
        weight = jnp.zeros((1, 1), jnp.float32)
        for vector in range(2 * vectors):
            force_bias = -STEP_ROOT * jnp.sum(total[vector] * weighted, keepdims=True)
            field = field_values[vector]
            increment += (STEP_ROOT * (field - force_bias)) * total[vector]
            weight += field * force_bias - 0.5 * force_bias * force_bias
        terms[pair] = increment.reshape(chol_count, own_rows, occ)
        weight = jnp.broadcast_to(weight, (LOG_ROWS, occ))
        tail = split(weight)
        for step, core in fars:
            target = 2 * to_high[step] + core
            far_out[pair, step, core, pl.ds(0, own_rows)] = terms[pair, target].astype(jnp.bfloat16)
            far_out[pair, step, core, pl.ds(own_rows, TAIL)] = tail
            far_copy(pair, step, core).start()
        sib_out[pair, pl.ds(0, own_rows)] = terms[pair, sibling]
        sib_out[pair, pl.ds(own_rows, LOG_ROWS)] = weight
        base[pair, low, pl.ds(0, own_rows)] = terms[pair, me]
        base[pair, low, pl.ds(own_rows, LOG_ROWS)] = weight
        sib_copy(pair).start()

    def split(weight):
        coarse = weight.astype(jnp.bfloat16).astype(jnp.float32)
        return jnp.concatenate([coarse, weight - coarse], axis=0).astype(jnp.bfloat16)

    def joined(tail):
        return tail[:LOG_ROWS] + tail[LOG_ROWS:]

    moved = [
        remote(moved_out, moved_in.at[bit], moved_send.at[bit], moved_recv.at[bit], {"walk": mates[bit]})
        for bit in range(bit_count)
    ]

    def finish(pair):
        cores = 1 if pair == home else 2

        def wait_sibling():
            remote(
                sib_out.at[pair],
                base.at[pair, 1 - low],
                sib_send.at[pair],
                sib_recv.at[pair],
                {"chol": sibling},
            ).wait_recv()

        if pair == home:
            pl.when(low == 1)(wait_sibling)
        else:
            wait_sibling()
        for step, core in fars:
            if core < cores:
                remote(
                    far_out.at[pair, step, core],
                    far_in.at[pair, step, core],
                    far_send.at[pair, step, core],
                    far_recv.at[pair, step, core],
                    {"chol": sibling},
                ).wait_recv()
        for core in range(cores):
            slot = 2 * pair + core
            rows_in = placed[pl.ds(0, own_rows)] if slot == LIVE - 1 else window[slot]
            result = rows_in.astype(jnp.float32) + base[pair, core, pl.ds(0, own_rows)]
            weight = base[pair, core, pl.ds(own_rows, LOG_ROWS)]
            for step in range(half - 1):
                result += far_in[pair, step, core, pl.ds(0, own_rows)].astype(jnp.float32)
                weight += joined(far_in[pair, step, core, pl.ds(own_rows, TAIL)].astype(jnp.float32))
            if slot < LIVE:
                done[slot] = result
                done_logs[slot] = weight
            else:
                moved_out[pl.ds(0, own_rows)] = result.astype(jnp.bfloat16)
                moved_out[pl.ds(own_rows, TAIL)] = split(weight)
        if pair == home:
            for copy in moved:
                begin(copy)

    pl.when(low == 0)(functools.partial(multiply, home))
    place_last()
    for pair in range(last):
        multiply(pair)
    near_copy(last, placed).wait_recv()
    own_half([last])
    finish(home)
    multiply(last)
    for pair in range(home):
        finish(pair)
    for copy in moved:
        copy.wait_recv()

    came_rows = arrived(lambda bit: moved_in[bit, pl.ds(0, own_rows)].astype(jnp.float32))
    came_logs = joined(arrived(lambda bit: moved_in[bit, pl.ds(own_rows, TAIL)].astype(jnp.float32)))

    def choose(slot, own, first, second):
        came_here = slot - own_count
        value = pick((came_here == 1) & (arriving > 1), second, jnp.zeros_like(own))
        value = pick((came_here == 0) & (arriving > 0), first, value)
        return pick(slot < jnp.minimum(own_count, LIVE), own, value)

    lane = lax.broadcasted_iota(jnp.int32, (LOG_ROWS, occ), 1)
    weights = jnp.zeros((LOG_ROWS, occ), jnp.float32)
    for slot in range(LIVE):
        new_out[slot] = choose(slot, done[slot], came_rows, done[LIVE - 1]).astype(jnp.bfloat16)
        weight = choose(slot, done_logs[slot], came_logs, done_logs[LIVE - 1])
        weights = jnp.where(lane == slot, weight, weights)
    log_out[...] = weights[0, :LIVE]

    for copy in sent:
        copy.wait_send()
    near_copy(last, placed).wait_send()
    for pair in range(home):
        sib_copy(pair).wait_send()
        for step, core in fars:
            far_copy(pair, step, core).wait_send()

    @pl.when(low == 0)
    def _():
        sib_copy(home).wait_send()
        for step, core in fars:
            far_copy(home, step, core).wait_send()

    @pl.when(low == 1)
    def _():
        near_copy(home, walkers.at[LIVE]).wait_send()


def shards(walkers, inv_intersection, fields, cholesky, trial_rows, counts, partner):
    chol_count = lax.axis_size("chol")
    bit_count = lax.axis_size("walk").bit_length() - 1
    slots, depth, occ = walkers.shape
    vectors, rows, orbitals = cholesky.shape
    own_rows = rows // chol_count
    others = chol_count // 2 - 1
    pairs = slots // 2
    field_rows = -(-slots * vectors // 16) * 16
    bf16, f32 = jnp.bfloat16, jnp.float32
    dma = pltpu.SemaphoreType.DMA
    anywhere = pl.BlockSpec(memory_space=pl.ANY)
    vmem = pl.BlockSpec(memory_space=pltpu.VMEM)
    operands = (walkers, inv_intersection, fields.T, cholesky, trial_rows, counts, partner)
    operands = [pltpu.with_memory_space_constraint(operand, pltpu.HBM) for operand in operands]
    return pl.pallas_call(
        functools.partial(kernel, chol_count, bit_count),
        out_shape=(
            jax.ShapeDtypeStruct((LIVE, own_rows, occ), bf16),
            jax.ShapeDtypeStruct((LIVE,), f32),
        ),
        in_specs=[anywhere, anywhere, vmem, anywhere, anywhere, anywhere, anywhere],
        out_specs=(vmem, vmem),
        scratch_shapes=[
            pltpu.SMEM(counts.shape, jnp.int32),
            pltpu.SMEM(partner.shape, jnp.int32),
            pltpu.VMEM((pairs, chol_count, depth, occ), bf16),
            pltpu.VMEM((slots, own_rows, occ), bf16),
            pltpu.VMEM((depth, occ), bf16),
            pltpu.VMEM((depth, occ), bf16),
            pltpu.VMEM((bit_count, depth, occ), bf16),
            pltpu.VMEM((2 * vectors, rows, orbitals), bf16),
            pltpu.VMEM((slots, occ, occ), bf16),
            pltpu.VMEM((bit_count, occ, occ), bf16),
            pltpu.VMEM((2, field_rows, occ), bf16),
            pltpu.VMEM((bit_count, 2, field_rows, occ), bf16),
            pltpu.VMEM((rows, occ), bf16),
            pltpu.VMEM((pairs, 2 * vectors * rows, occ), f32),
            pltpu.VMEM((pairs, chol_count, own_rows, occ), f32),
            pltpu.VMEM((pairs, 2, own_rows + LOG_ROWS, occ), f32),
            pltpu.VMEM((pairs, own_rows + LOG_ROWS, occ), f32),
            pltpu.VMEM((pairs, others, 2, own_rows + TAIL, occ), bf16),
            pltpu.VMEM((pairs, others, 2, own_rows + TAIL, occ), bf16),
            pltpu.VMEM((LIVE, own_rows, occ), f32),
            pltpu.VMEM((LIVE, LOG_ROWS, occ), f32),
            pltpu.VMEM((own_rows + TAIL, occ), bf16),
            pltpu.VMEM((bit_count, own_rows + TAIL, occ), bf16),
            dma((7 + pairs,)),
            dma((3, bit_count)),
            dma((3, bit_count)),
            dma((2,)),
            dma((2,)),
            dma((pairs,)),
            dma((pairs,)),
            dma((pairs, others, 2)),
            dma((pairs, others, 2)),
            dma((pairs,)),
            dma((pairs,)),
            dma((pairs, others, 2)),
            dma((pairs, others, 2)),
            dma((bit_count,)),
            dma((bit_count,)),
        ],
        compiler_params=pltpu.CompilerParams(
            collective_id=0, has_side_effects=True, vmem_limit_bytes=VMEM_BYTES
        ),
        cost_estimate=pl.CostEstimate(
            flops=2 * slots * vectors * rows * orbitals * occ,
            bytes_accessed=2 * (walkers.size + cholesky.size),
            transcendentals=0,
        ),
    )(*operands)


def solution(mesh):
    in_specs = (
        P("walk", "chol", None),
        P("walk", None, None),
        P("walk", "chol"),
        P("chol", None, None),
        P(),
        P(),
        P(),
    )
    out_specs = (P("walk", "chol", None), P("walk"))
    return jax.shard_map(shards, mesh=mesh, in_specs=in_specs, out_specs=out_specs, check_vma=False)
```

```python
import functools

import jax
import jax.numpy as jnp
from jax import lax
from jax.experimental import pallas as pl
from jax.experimental.pallas import tpu as pltpu
from jax.sharding import PartitionSpec as P

LIVE = 4
VMEM_BYTES = 40 << 20
STEP_ROOT = 0.1
LOG_ROWS = 8
TAIL = 2 * LOG_ROWS
MESH = pl.DeviceIdType.MESH


def pick(flag, chosen, other):
    mask = jnp.broadcast_to(flag.astype(jnp.int32), chosen.shape) > 0
    return jnp.where(mask, chosen, other)


def kernel(
    chol_count,
    bit_count,
    walkers,
    minv_in,
    fields,
    chol_in,
    trial_in,
    counts_in,
    partner_in,
    new_out,
    log_out,
    counts,
    partner,
    phi,
    window,
    kept,
    placed,
    came,
    chol,
    minv,
    came_minv,
    field_all,
    came_field,
    trial,
    prod,
    terms,
    base,
    sib_out,
    far_out,
    far_in,
    done,
    done_logs,
    moved_out,
    moved_in,
    load_sem,
    came_send,
    came_recv,
    swap_send,
    swap_recv,
    near_send,
    near_recv,
    ahead_send,
    ahead_recv,
    sib_send,
    sib_recv,
    far_send,
    far_recv,
    moved_send,
    moved_recv,
):
    slots, depth, occ = walkers.shape
    vectors, rows, _ = chol_in.shape
    own_rows = rows // chol_count
    half = chol_count // 2
    pairs = slots // 2
    walk = lax.axis_index("walk")
    me = lax.axis_index("chol")
    high, low = me // 2, me % 2
    sibling = 2 * high + 1 - low
    to_high = [lax.rem(high + step, half) for step in range(1, half)]
    from_high = [lax.rem(high - step + half, half) for step in range(1, half)]
    mates = [jnp.bitwise_xor(walk, 1 << bit) for bit in range(bit_count)]
    fars = [(step, core) for step in range(half - 1) for core in range(2)]

    loads = [
        pltpu.make_async_copy(chol_in, chol.at[pl.ds(low * vectors, vectors)], load_sem.at[0]),
        pltpu.make_async_copy(minv_in, minv, load_sem.at[1]),
        pltpu.make_async_copy(trial_in, trial, load_sem.at[2]),
        pltpu.make_async_copy(walkers.at[:, pl.ds(0, own_rows)], window, load_sem.at[3]),
        pltpu.make_async_copy(walkers.at[LIVE - 1], kept, load_sem.at[4 + pairs]),
    ]
    table_loads = [
        pltpu.make_async_copy(counts_in, counts, load_sem.at[5 + pairs]),
        pltpu.make_async_copy(partner_in, partner, load_sem.at[6 + pairs]),
    ]
    own_loads = [
        pltpu.make_async_copy(walkers.at[2 * pair + low], phi.at[pair, me], load_sem.at[4 + pair])
        for pair in range(pairs)
    ]
    for load in loads + own_loads + table_loads:
        load.start()

    barrier = pltpu.get_barrier_semaphore()
    peers = [{"chol": sibling}] + [{"chol": 2 * to_high[step] + core} for step, core in fars]
    peers += [{"walk": mate} for mate in mates]
    for peer in peers:
        pl.semaphore_signal(barrier, inc=1, device_id=peer, device_id_type=MESH)

    field_wide = fields[...].astype(jnp.float32)
    line = lax.broadcasted_iota(jnp.int32, field_all.shape[1:], 0)
    spread = jnp.zeros(field_all.shape[1:], jnp.float32)
    for slot in range(slots):
        for vector in range(vectors):
            value = field_wide[vector : vector + 1, slot : slot + 1]
            spread = jnp.where(line == slot * vectors + vector, value, spread)
    field_all[low] = spread.astype(jnp.bfloat16)

    pl.semaphore_wait(barrier, len(peers))

    def remote(src, dst, send, recv, peer):
        return pltpu.make_async_remote_copy(
            src_ref=src, dst_ref=dst, send_sem=send, recv_sem=recv, device_id=peer, device_id_type=MESH
        )

    sent = []

    def begin(copy):
        copy.start()
        sent.append(copy)
        return copy

    def send_ahead(slot, source):
        for step in range(half - 1):
            begin(
                remote(
                    source,
                    phi.at[slot // 2, me],
                    ahead_send.at[slot // 2, step, slot % 2],
                    ahead_recv.at[slot // 2, step, low],
                    {"chol": 2 * to_high[step] + slot % 2},
                )
            )

    def wait_ahead(pair):
        for step, core in fars:
            remote(
                walkers.at[0],
                phi.at[pair, 2 * from_high[step] + core],
                ahead_send.at[pair, step, core],
                ahead_recv.at[pair, step, core],
                {"chol": sibling},
            ).wait_recv()

    def near_copy(pair, source):
        return remote(source, phi.at[pair, me], near_send.at[pair], near_recv.at[pair], {"chol": sibling})

    home, last = LIVE // 2, LIVE // 2 - 1
    send_ahead(LIVE, walkers.at[LIVE])
    moves = [
        begin(
            remote(
                walkers.at[LIVE + 1],
                came.at[bit],
                came_send.at[0, bit],
                came_recv.at[0, bit],
                {"walk": mates[bit]},
            )
        )
        for bit in reversed(range(bit_count))
    ]
    send_ahead(0, walkers.at[0])
    send_ahead(1, walkers.at[1])
    swaps = [
        begin(remote(field_all.at[low], field_all.at[low], swap_send.at[0], swap_recv.at[0], {"chol": sibling})),
    ]

    def swap(step):
        start = lax.rem(high + step, half) * 2 * depth
        columns = pl.ds(pl.multiple_of(start, 2 * depth), 2 * depth)
        return remote(
            chol_in.at[:, :, columns],
            chol.at[pl.ds(low * vectors, vectors), :, columns],
            swap_send.at[1 + step],
            swap_recv.at[1 + step],
            {"chol": sibling},
        )

    swaps += [begin(swap(0))]
    near = [near_copy(pair, walkers.at[2 * pair + 1 - low]) for pair in range(last)]
    for copy in near:
        begin(copy)

    @pl.when(low == 1)
    def _():
        near_copy(home, walkers.at[LIVE]).start()
        near_copy(last, walkers.at[LIVE - 2]).start()

    swaps += [begin(swap(step)) for step in range(1, half)]
    moves += [
        begin(
            remote(
                minv_in.at[LIVE + 1],
                came_minv.at[bit],
                came_send.at[1, bit],
                came_recv.at[1, bit],
                {"walk": mates[bit]},
            )
        )
        for bit in range(bit_count)
    ]
    swaps[0].wait_recv()
    moves += [
        begin(
            remote(
                field_all,
                came_field.at[bit],
                came_send.at[2, bit],
                came_recv.at[2, bit],
                {"walk": mates[bit]},
            )
        )
        for bit in range(bit_count)
    ]

    for load in table_loads:
        load.wait()
    mate = partner[walk]
    own_count = counts[walk]
    arriving = jnp.maximum(counts[mate] - LIVE, 0)
    distance = jnp.bitwise_xor(mate, walk)

    def arrived(read):
        value = read(0)
        for bit in range(1, bit_count):
            value = pick(distance == 1 << bit, read(bit), value)
        return value

    def place(own, read):
        return pick(own_count < LIVE, arrived(read), own)

    def chol_half(index):
        columns = pl.ds(pl.multiple_of(index * 2 * depth, 2 * depth), 2 * depth)
        return chol[:, :, columns].reshape(2 * vectors * rows, 2 * depth)

    def phi_half(pair, index):
        return phi[pair, pl.ds(2 * index, 2)].reshape(2 * depth, occ)

    for load in loads + own_loads:
        load.wait()
    for copy in near + swaps[1:2]:
        copy.wait_recv()

    @pl.when(low == 0)
    def _():
        near_copy(home, walkers.at[LIVE]).wait_recv()

    def own_half(some):
        every = jnp.concatenate([phi_half(pair, high) for pair in some], axis=1)
        result = jnp.dot(chol_half(high), every, preferred_element_type=jnp.float32)
        for index, pair in enumerate(some):
            prod[pair] = result[:, index * occ : (index + 1) * occ]

    own_half([home] + list(range(last)))
    for copy in swaps[2:]:
        copy.wait_recv()

    def place_last():
        send_ahead(LIVE - 2, walkers.at[LIVE - 2])
        for copy in moves:
            copy.wait_recv()
        placed[...] = place(kept[...], lambda bit: came[bit])
        send_ahead(LIVE - 1, placed)

        @pl.when(low == 0)
        def _():
            near_copy(last, placed).start()

        phi[last, me] = pick(low == 1, placed[...], phi[last, me])

    def field_of(pair, vector):
        values = field_all[vector // vectors].astype(jnp.float32)
        place_in = vector % vectors

        def at(array, slot):
            line = slot * vectors + place_in
            return array[line : line + 1, :1]

        second = at(values, 2 * pair + 1)
        if pair == last:
            second = place(
                second, lambda bit: at(came_field[bit, vector // vectors].astype(jnp.float32), LIVE + 1)
            )
        return pick(low == 0, at(values, 2 * pair), second)

    def far_copy(pair, step, core):
        return remote(
            far_out.at[pair, step, core],
            far_in.at[pair, step, low],
            far_send.at[pair, step, core],
            far_recv.at[pair, step, low],
            {"chol": 2 * to_high[step] + core},
        )

    def sib_copy(pair):
        return remote(
            sib_out.at[pair], base.at[pair, low], sib_send.at[pair], sib_recv.at[pair], {"chol": sibling}
        )

    def multiply(pair):
        inverse = minv[2 * pair + low]
        if pair == last:
            inverse = pick(low == 0, inverse, place(minv[LIVE - 1], lambda bit: came_minv[bit]))
        weighted = lax.dot_general(
            trial[...], inverse, (((1,), (1,)), ((), ())), preferred_element_type=jnp.float32
        )
        field_values = [field_of(pair, vector) for vector in range(2 * vectors)]
        wait_ahead(pair)
        total = prod[pair]
        for step in range(half - 1):
            total += jnp.dot(
                chol_half(from_high[step]),
                phi_half(pair, from_high[step]),
                preferred_element_type=jnp.float32,
            )
        total = total.reshape(2 * vectors, rows, occ)
        increment = jnp.zeros((rows, occ), jnp.float32)
        weight = jnp.zeros((1, 1), jnp.float32)
        for vector in range(2 * vectors):
            force_bias = -STEP_ROOT * jnp.sum(total[vector] * weighted, keepdims=True)
            field = field_values[vector]
            increment += (STEP_ROOT * (field - force_bias)) * total[vector]
            weight += field * force_bias - 0.5 * force_bias * force_bias
        terms[pair] = increment.reshape(chol_count, own_rows, occ)
        weight = jnp.broadcast_to(weight, (LOG_ROWS, occ))
        tail = split(weight)
        for step, core in fars:
            target = 2 * to_high[step] + core
            far_out[pair, step, core, pl.ds(0, own_rows)] = terms[pair, target].astype(jnp.bfloat16)
            far_out[pair, step, core, pl.ds(own_rows, TAIL)] = tail
            far_copy(pair, step, core).start()
        sib_out[pair, pl.ds(0, own_rows)] = terms[pair, sibling]
        sib_out[pair, pl.ds(own_rows, LOG_ROWS)] = weight
        base[pair, low, pl.ds(0, own_rows)] = terms[pair, me]
        base[pair, low, pl.ds(own_rows, LOG_ROWS)] = weight
        sib_copy(pair).start()

    def split(weight):
        coarse = weight.astype(jnp.bfloat16).astype(jnp.float32)
        return jnp.concatenate([coarse, weight - coarse], axis=0).astype(jnp.bfloat16)

    def joined(tail):
        return tail[:LOG_ROWS] + tail[LOG_ROWS:]

    moved = [
        remote(moved_out, moved_in.at[bit], moved_send.at[bit], moved_recv.at[bit], {"walk": mates[bit]})
        for bit in range(bit_count)
    ]

    def finish(pair):
        cores = 1 if pair == home else 2

        def wait_sibling():
            remote(
                sib_out.at[pair],
                base.at[pair, 1 - low],
                sib_send.at[pair],
                sib_recv.at[pair],
                {"chol": sibling},
            ).wait_recv()

        if pair == home:
            pl.when(low == 1)(wait_sibling)
        else:
            wait_sibling()
        for step, core in fars:
            if core < cores:
                remote(
                    far_out.at[pair, step, core],
                    far_in.at[pair, step, core],
                    far_send.at[pair, step, core],
                    far_recv.at[pair, step, core],
                    {"chol": sibling},
                ).wait_recv()
        for core in range(cores):
            slot = 2 * pair + core
            rows_in = placed[pl.ds(0, own_rows)] if slot == LIVE - 1 else window[slot]
            result = rows_in.astype(jnp.float32) + base[pair, core, pl.ds(0, own_rows)]
            weight = base[pair, core, pl.ds(own_rows, LOG_ROWS)]
            for step in range(half - 1):
                result += far_in[pair, step, core, pl.ds(0, own_rows)].astype(jnp.float32)
                weight += joined(far_in[pair, step, core, pl.ds(own_rows, TAIL)].astype(jnp.float32))
            if slot < LIVE:
                done[slot] = result
                done_logs[slot] = weight
            else:
                moved_out[pl.ds(0, own_rows)] = result.astype(jnp.bfloat16)
                moved_out[pl.ds(own_rows, TAIL)] = split(weight)
        if pair == home:
            for copy in moved:
                begin(copy)

    pl.when(low == 0)(functools.partial(multiply, home))
    place_last()
    for pair in range(last):
        multiply(pair)
    near_copy(last, placed).wait_recv()
    own_half([last])
    finish(home)
    multiply(last)
    for pair in range(home):
        finish(pair)
    for copy in moved:
        copy.wait_recv()

    came_rows = arrived(lambda bit: moved_in[bit, pl.ds(0, own_rows)].astype(jnp.float32))
    came_logs = joined(arrived(lambda bit: moved_in[bit, pl.ds(own_rows, TAIL)].astype(jnp.float32)))

    def choose(slot, own, first, second):
        came_here = slot - own_count
        value = pick((came_here == 1) & (arriving > 1), second, jnp.zeros_like(own))
        value = pick((came_here == 0) & (arriving > 0), first, value)
        return pick(slot < jnp.minimum(own_count, LIVE), own, value)

    lane = lax.broadcasted_iota(jnp.int32, (LOG_ROWS, occ), 1)
    weights = jnp.zeros((LOG_ROWS, occ), jnp.float32)
    for slot in range(LIVE):
        new_out[slot] = choose(slot, done[slot], came_rows, done[LIVE - 1]).astype(jnp.bfloat16)
        weight = choose(slot, done_logs[slot], came_logs, done_logs[LIVE - 1])
        weights = jnp.where(lane == slot, weight, weights)
    log_out[...] = weights[0, :LIVE]

    for copy in sent:
        copy.wait_send()
    near_copy(last, placed).wait_send()
    for pair in range(home):
        sib_copy(pair).wait_send()
        for step, core in fars:
            far_copy(pair, step, core).wait_send()

    @pl.when(low == 0)
    def _():
        sib_copy(home).wait_send()
        for step, core in fars:
            far_copy(home, step, core).wait_send()

    @pl.when(low == 1)
    def _():
        near_copy(home, walkers.at[LIVE]).wait_send()


def shards(walkers, inv_intersection, fields, cholesky, trial_rows, counts, partner):
    chol_count = lax.axis_size("chol")
    bit_count = lax.axis_size("walk").bit_length() - 1
    slots, depth, occ = walkers.shape
    vectors, rows, orbitals = cholesky.shape
    own_rows = rows // chol_count
    others = chol_count // 2 - 1
    pairs = slots // 2
    field_rows = -(-slots * vectors // 16) * 16
    bf16, f32 = jnp.bfloat16, jnp.float32
    dma = pltpu.SemaphoreType.DMA
    anywhere = pl.BlockSpec(memory_space=pl.ANY)
    vmem = pl.BlockSpec(memory_space=pltpu.VMEM)
    operands = (walkers, inv_intersection, fields.T, cholesky, trial_rows, counts, partner)
    operands = [pltpu.with_memory_space_constraint(operand, pltpu.HBM) for operand in operands]
    return pl.pallas_call(
        functools.partial(kernel, chol_count, bit_count),
        out_shape=(
            jax.ShapeDtypeStruct((LIVE, own_rows, occ), bf16),
            jax.ShapeDtypeStruct((LIVE,), f32),
        ),
        in_specs=[anywhere, anywhere, vmem, anywhere, anywhere, anywhere, anywhere],
        out_specs=(vmem, vmem),
        scratch_shapes=[
            pltpu.SMEM(counts.shape, jnp.int32),
            pltpu.SMEM(partner.shape, jnp.int32),
            pltpu.VMEM((pairs, chol_count, depth, occ), bf16),
            pltpu.VMEM((slots, own_rows, occ), bf16),
            pltpu.VMEM((depth, occ), bf16),
            pltpu.VMEM((depth, occ), bf16),
            pltpu.VMEM((bit_count, depth, occ), bf16),
            pltpu.VMEM((2 * vectors, rows, orbitals), bf16),
            pltpu.VMEM((slots, occ, occ), bf16),
            pltpu.VMEM((bit_count, occ, occ), bf16),
            pltpu.VMEM((2, field_rows, occ), bf16),
            pltpu.VMEM((bit_count, 2, field_rows, occ), bf16),
            pltpu.VMEM((rows, occ), bf16),
            pltpu.VMEM((pairs, 2 * vectors * rows, occ), f32),
            pltpu.VMEM((pairs, chol_count, own_rows, occ), f32),
            pltpu.VMEM((pairs, 2, own_rows + LOG_ROWS, occ), f32),
            pltpu.VMEM((pairs, own_rows + LOG_ROWS, occ), f32),
            pltpu.VMEM((pairs, others, 2, own_rows + TAIL, occ), bf16),
            pltpu.VMEM((pairs, others, 2, own_rows + TAIL, occ), bf16),
            pltpu.VMEM((LIVE, own_rows, occ), f32),
            pltpu.VMEM((LIVE, LOG_ROWS, occ), f32),
            pltpu.VMEM((own_rows + TAIL, occ), bf16),
            pltpu.VMEM((bit_count, own_rows + TAIL, occ), bf16),
            dma((7 + pairs,)),
            dma((3, bit_count)),
            dma((3, bit_count)),
            dma((1 + chol_count // 2,)),
            dma((1 + chol_count // 2,)),
            dma((pairs,)),
            dma((pairs,)),
            dma((pairs, others, 2)),
            dma((pairs, others, 2)),
            dma((pairs,)),
            dma((pairs,)),
            dma((pairs, others, 2)),
            dma((pairs, others, 2)),
            dma((bit_count,)),
            dma((bit_count,)),
        ],
        compiler_params=pltpu.CompilerParams(
            collective_id=0, has_side_effects=True, vmem_limit_bytes=VMEM_BYTES
        ),
        cost_estimate=pl.CostEstimate(
            flops=2 * slots * vectors * rows * orbitals * occ,
            bytes_accessed=2 * (walkers.size + cholesky.size),
            transcendentals=0,
        ),
    )(*operands)


def solution(mesh):
    in_specs = (
        P("walk", "chol", None),
        P("walk", None, None),
        P("walk", "chol"),
        P("chol", None, None),
        P(),
        P(),
        P(),
    )
    out_specs = (P("walk", "chol", None), P("walk"))
    return jax.shard_map(shards, mesh=mesh, in_specs=in_specs, out_specs=out_specs, check_vma=False)
```

```python
import functools

import jax
import jax.numpy as jnp
from jax import lax
from jax.experimental import pallas as pl
from jax.experimental.pallas import tpu as pltpu
from jax.sharding import PartitionSpec as P

LIVE = 4
VMEM_BYTES = 40 << 20
STEP_ROOT = 0.1
LOG_ROWS = 8
TAIL = 2 * LOG_ROWS
MESH = pl.DeviceIdType.MESH


def pick(flag, chosen, other):
    mask = jnp.broadcast_to(flag.astype(jnp.int32), chosen.shape) > 0
    return jnp.where(mask, chosen, other)


def kernel(
    chol_count,
    bit_count,
    walkers,
    minv_in,
    fields,
    chol_in,
    trial_in,
    counts_in,
    partner_in,
    new_out,
    log_out,
    counts,
    partner,
    phi,
    window,
    kept,
    placed,
    came,
    chol,
    minv,
    came_minv,
    field_all,
    came_field,
    trial,
    prod,
    terms,
    base,
    sib_out,
    far_out,
    far_in,
    done,
    done_logs,
    moved_out,
    moved_in,
    load_sem,
    came_send,
    came_recv,
    swap_send,
    swap_recv,
    near_send,
    near_recv,
    ahead_send,
    ahead_recv,
    sib_send,
    sib_recv,
    far_send,
    far_recv,
    moved_send,
    moved_recv,
):
    slots, depth, occ = walkers.shape
    vectors, rows, _ = chol_in.shape
    own_rows = rows // chol_count
    half = chol_count // 2
    pairs = slots // 2
    walk = lax.axis_index("walk")
    me = lax.axis_index("chol")
    high, low = me // 2, me % 2
    sibling = 2 * high + 1 - low
    to_high = [lax.rem(high + step, half) for step in range(1, half)]
    from_high = [lax.rem(high - step + half, half) for step in range(1, half)]
    mates = [jnp.bitwise_xor(walk, 1 << bit) for bit in range(bit_count)]
    fars = [(step, core) for step in range(half - 1) for core in range(2)]

    loads = [
        pltpu.make_async_copy(chol_in, chol.at[pl.ds(low * vectors, vectors)], load_sem.at[0]),
        pltpu.make_async_copy(minv_in, minv, load_sem.at[1]),
        pltpu.make_async_copy(trial_in, trial, load_sem.at[2]),
        pltpu.make_async_copy(walkers.at[:, pl.ds(0, own_rows)], window, load_sem.at[3]),
        pltpu.make_async_copy(walkers.at[LIVE - 1], kept, load_sem.at[4 + pairs]),
    ]
    table_loads = [
        pltpu.make_async_copy(counts_in, counts, load_sem.at[5 + pairs]),
        pltpu.make_async_copy(partner_in, partner, load_sem.at[6 + pairs]),
    ]
    own_loads = [
        pltpu.make_async_copy(walkers.at[2 * pair + low], phi.at[pair, me], load_sem.at[4 + pair])
        for pair in range(pairs)
    ]
    for load in loads + own_loads + table_loads:
        load.start()

    barrier = pltpu.get_barrier_semaphore()
    peers = [{"chol": sibling}] + [{"chol": 2 * to_high[step] + core} for step, core in fars]
    peers += [{"walk": mate} for mate in mates]
    for peer in peers:
        pl.semaphore_signal(barrier, inc=1, device_id=peer, device_id_type=MESH)

    field_wide = fields[...].astype(jnp.float32)
    line = lax.broadcasted_iota(jnp.int32, field_all.shape[1:], 0)
    spread = jnp.zeros(field_all.shape[1:], jnp.float32)
    for slot in range(slots):
        for vector in range(vectors):
            value = field_wide[vector : vector + 1, slot : slot + 1]
            spread = jnp.where(line == slot * vectors + vector, value, spread)
    field_all[low] = spread.astype(jnp.bfloat16)

    pl.semaphore_wait(barrier, len(peers))

    def remote(src, dst, send, recv, peer):
        return pltpu.make_async_remote_copy(
            src_ref=src, dst_ref=dst, send_sem=send, recv_sem=recv, device_id=peer, device_id_type=MESH
        )

    sent = []

    def begin(copy):
        copy.start()
        sent.append(copy)
        return copy

    def send_ahead(slot, source):
        for step in range(half - 1):
            begin(
                remote(
                    source,
                    phi.at[slot // 2, me],
                    ahead_send.at[slot // 2, step, slot % 2],
                    ahead_recv.at[slot // 2, step, low],
                    {"chol": 2 * to_high[step] + slot % 2},
                )
            )

    def wait_ahead(pair):
        for step, core in fars:
            remote(
                walkers.at[0],
                phi.at[pair, 2 * from_high[step] + core],
                ahead_send.at[pair, step, core],
                ahead_recv.at[pair, step, core],
                {"chol": sibling},
            ).wait_recv()

    def near_copy(pair, source):
        return remote(source, phi.at[pair, me], near_send.at[pair], near_recv.at[pair], {"chol": sibling})

    home, last = LIVE // 2, LIVE // 2 - 1
    send_ahead(LIVE, walkers.at[LIVE])
    moves = [
        begin(
            remote(
                walkers.at[LIVE + 1],
                came.at[bit],
                came_send.at[0, bit],
                came_recv.at[0, bit],
                {"walk": mates[bit]},
            )
        )
        for bit in reversed(range(bit_count))
    ]
    send_ahead(0, walkers.at[0])
    send_ahead(1, walkers.at[1])
    swaps = [
        begin(remote(field_all.at[low], field_all.at[low], swap_send.at[0], swap_recv.at[0], {"chol": sibling})),
    ]

    def swap(step):
        start = lax.rem(high + step, half) * 2 * depth
        columns = pl.ds(pl.multiple_of(start, 2 * depth), 2 * depth)
        return remote(
            chol_in.at[:, :, columns],
            chol.at[pl.ds(low * vectors, vectors), :, columns],
            swap_send.at[1 + step],
            swap_recv.at[1 + step],
            {"chol": sibling},
        )

    swaps += [begin(swap(0))]
    near = [near_copy(pair, walkers.at[2 * pair + 1 - low]) for pair in range(last)]
    for copy in near:
        begin(copy)

    @pl.when(low == 1)
    def _():
        near_copy(home, walkers.at[LIVE]).start()
        near_copy(last, walkers.at[LIVE - 2]).start()

    swaps += [begin(swap(step)) for step in range(1, half)]
    moves += [
        begin(
            remote(
                minv_in.at[LIVE + 1],
                came_minv.at[bit],
                came_send.at[1, bit],
                came_recv.at[1, bit],
                {"walk": mates[bit]},
            )
        )
        for bit in range(bit_count)
    ]
    swaps[0].wait_recv()
    moves += [
        begin(
            remote(
                field_all,
                came_field.at[bit],
                came_send.at[2, bit],
                came_recv.at[2, bit],
                {"walk": mates[bit]},
            )
        )
        for bit in range(bit_count)
    ]

    for load in table_loads:
        load.wait()
    mate = partner[walk]
    own_count = counts[walk]
    arriving = jnp.maximum(counts[mate] - LIVE, 0)
    distance = jnp.bitwise_xor(mate, walk)

    def arrived(read):
        value = read(0)
        for bit in range(1, bit_count):
            value = pick(distance == 1 << bit, read(bit), value)
        return value

    def place(own, read):
        return pick(own_count < LIVE, arrived(read), own)

    def chol_half(index):
        columns = pl.ds(pl.multiple_of(index * 2 * depth, 2 * depth), 2 * depth)
        return chol[:, :, columns].reshape(2 * vectors * rows, 2 * depth)

    def phi_half(pair, index):
        return phi[pair, pl.ds(2 * index, 2)].reshape(2 * depth, occ)

    for load in loads + own_loads:
        load.wait()
    for copy in near + swaps[1:2]:
        copy.wait_recv()

    @pl.when(low == 0)
    def _():
        near_copy(home, walkers.at[LIVE]).wait_recv()

    def own_half(some):
        every = jnp.concatenate([phi_half(pair, high) for pair in some], axis=1)
        result = jnp.dot(chol_half(high), every, preferred_element_type=jnp.float32)
        for index, pair in enumerate(some):
            prod[pair] = result[:, index * occ : (index + 1) * occ]

    own_half([home] + list(range(last)))
    for copy in swaps[2:]:
        copy.wait_recv()

    def place_last():
        send_ahead(LIVE - 2, walkers.at[LIVE - 2])
        for copy in moves[:bit_count]:
            copy.wait_recv()
        placed[...] = place(kept[...], lambda bit: came[bit])
        send_ahead(LIVE - 1, placed)

        @pl.when(low == 0)
        def _():
            near_copy(last, placed).start()

        phi[last, me] = pick(low == 1, placed[...], phi[last, me])

    def field_of(pair, vector):
        values = field_all[vector // vectors].astype(jnp.float32)
        place_in = vector % vectors

        def at(array, slot):
            line = slot * vectors + place_in
            return array[line : line + 1, :1]

        second = at(values, 2 * pair + 1)
        if pair == last:
            second = place(
                second, lambda bit: at(came_field[bit, vector // vectors].astype(jnp.float32), LIVE + 1)
            )
        return pick(low == 0, at(values, 2 * pair), second)

    def far_copy(pair, step, core):
        return remote(
            far_out.at[pair, step, core],
            far_in.at[pair, step, low],
            far_send.at[pair, step, core],
            far_recv.at[pair, step, low],
            {"chol": 2 * to_high[step] + core},
        )

    def sib_copy(pair):
        return remote(
            sib_out.at[pair], base.at[pair, low], sib_send.at[pair], sib_recv.at[pair], {"chol": sibling}
        )

    def multiply(pair):
        inverse = minv[2 * pair + low]
        if pair == last:
            inverse = pick(low == 0, inverse, place(minv[LIVE - 1], lambda bit: came_minv[bit]))
        weighted = lax.dot_general(
            trial[...], inverse, (((1,), (1,)), ((), ())), preferred_element_type=jnp.float32
        )
        field_values = [field_of(pair, vector) for vector in range(2 * vectors)]
        wait_ahead(pair)
        total = prod[pair]
        for step in range(half - 1):
            total += jnp.dot(
                chol_half(from_high[step]),
                phi_half(pair, from_high[step]),
                preferred_element_type=jnp.float32,
            )
        total = total.reshape(2 * vectors, rows, occ)
        increment = jnp.zeros((rows, occ), jnp.float32)
        weight = jnp.zeros((1, 1), jnp.float32)
        for vector in range(2 * vectors):
            force_bias = -STEP_ROOT * jnp.sum(total[vector] * weighted, keepdims=True)
            field = field_values[vector]
            increment += (STEP_ROOT * (field - force_bias)) * total[vector]
            weight += field * force_bias - 0.5 * force_bias * force_bias
        terms[pair] = increment.reshape(chol_count, own_rows, occ)
        weight = jnp.broadcast_to(weight, (LOG_ROWS, occ))
        tail = split(weight)
        for step, core in fars:
            target = 2 * to_high[step] + core
            far_out[pair, step, core, pl.ds(0, own_rows)] = terms[pair, target].astype(jnp.bfloat16)
            far_out[pair, step, core, pl.ds(own_rows, TAIL)] = tail
            far_copy(pair, step, core).start()
        sib_out[pair, pl.ds(0, own_rows)] = terms[pair, sibling]
        sib_out[pair, pl.ds(own_rows, LOG_ROWS)] = weight
        base[pair, low, pl.ds(0, own_rows)] = terms[pair, me]
        base[pair, low, pl.ds(own_rows, LOG_ROWS)] = weight
        sib_copy(pair).start()

    def split(weight):
        coarse = weight.astype(jnp.bfloat16).astype(jnp.float32)
        return jnp.concatenate([coarse, weight - coarse], axis=0).astype(jnp.bfloat16)

    def joined(tail):
        return tail[:LOG_ROWS] + tail[LOG_ROWS:]

    moved = [
        remote(moved_out, moved_in.at[bit], moved_send.at[bit], moved_recv.at[bit], {"walk": mates[bit]})
        for bit in range(bit_count)
    ]

    def finish(pair):
        cores = 1 if pair == home else 2

        def wait_sibling():
            remote(
                sib_out.at[pair],
                base.at[pair, 1 - low],
                sib_send.at[pair],
                sib_recv.at[pair],
                {"chol": sibling},
            ).wait_recv()

        if pair == home:
            pl.when(low == 1)(wait_sibling)
        else:
            wait_sibling()
        for step, core in fars:
            if core < cores:
                remote(
                    far_out.at[pair, step, core],
                    far_in.at[pair, step, core],
                    far_send.at[pair, step, core],
                    far_recv.at[pair, step, core],
                    {"chol": sibling},
                ).wait_recv()
        for core in range(cores):
            slot = 2 * pair + core
            rows_in = placed[pl.ds(0, own_rows)] if slot == LIVE - 1 else window[slot]
            result = rows_in.astype(jnp.float32) + base[pair, core, pl.ds(0, own_rows)]
            weight = base[pair, core, pl.ds(own_rows, LOG_ROWS)]
            for step in range(half - 1):
                result += far_in[pair, step, core, pl.ds(0, own_rows)].astype(jnp.float32)
                weight += joined(far_in[pair, step, core, pl.ds(own_rows, TAIL)].astype(jnp.float32))
            if slot < LIVE:
                done[slot] = result
                done_logs[slot] = weight
            else:
                moved_out[pl.ds(0, own_rows)] = result.astype(jnp.bfloat16)
                moved_out[pl.ds(own_rows, TAIL)] = split(weight)
        if pair == home:
            for copy in moved:
                begin(copy)

    pl.when(low == 0)(functools.partial(multiply, home))
    place_last()
    for pair in range(last):
        multiply(pair)
    near_copy(last, placed).wait_recv()
    own_half([last])
    finish(home)
    for copy in moves[bit_count:]:
        copy.wait_recv()
    multiply(last)
    for pair in range(home):
        finish(pair)
    for copy in moved:
        copy.wait_recv()

    came_rows = arrived(lambda bit: moved_in[bit, pl.ds(0, own_rows)].astype(jnp.float32))
    came_logs = joined(arrived(lambda bit: moved_in[bit, pl.ds(own_rows, TAIL)].astype(jnp.float32)))

    def choose(slot, own, first, second):
        came_here = slot - own_count
        value = pick((came_here == 1) & (arriving > 1), second, jnp.zeros_like(own))
        value = pick((came_here == 0) & (arriving > 0), first, value)
        return pick(slot < jnp.minimum(own_count, LIVE), own, value)

    lane = lax.broadcasted_iota(jnp.int32, (LOG_ROWS, occ), 1)
    weights = jnp.zeros((LOG_ROWS, occ), jnp.float32)
    for slot in range(LIVE):
        new_out[slot] = choose(slot, done[slot], came_rows, done[LIVE - 1]).astype(jnp.bfloat16)
        weight = choose(slot, done_logs[slot], came_logs, done_logs[LIVE - 1])
        weights = jnp.where(lane == slot, weight, weights)
    log_out[...] = weights[0, :LIVE]

    for copy in sent:
        copy.wait_send()
    near_copy(last, placed).wait_send()
    for pair in range(home):
        sib_copy(pair).wait_send()
        for step, core in fars:
            far_copy(pair, step, core).wait_send()

    @pl.when(low == 0)
    def _():
        sib_copy(home).wait_send()
        for step, core in fars:
            far_copy(home, step, core).wait_send()

    @pl.when(low == 1)
    def _():
        near_copy(home, walkers.at[LIVE]).wait_send()


def shards(walkers, inv_intersection, fields, cholesky, trial_rows, counts, partner):
    chol_count = lax.axis_size("chol")
    bit_count = lax.axis_size("walk").bit_length() - 1
    slots, depth, occ = walkers.shape
    vectors, rows, orbitals = cholesky.shape
    own_rows = rows // chol_count
    others = chol_count // 2 - 1
    pairs = slots // 2
    field_rows = -(-slots * vectors // 16) * 16
    bf16, f32 = jnp.bfloat16, jnp.float32
    dma = pltpu.SemaphoreType.DMA
    anywhere = pl.BlockSpec(memory_space=pl.ANY)
    vmem = pl.BlockSpec(memory_space=pltpu.VMEM)
    operands = (walkers, inv_intersection, fields.T, cholesky, trial_rows, counts, partner)
    operands = [pltpu.with_memory_space_constraint(operand, pltpu.HBM) for operand in operands]
    return pl.pallas_call(
        functools.partial(kernel, chol_count, bit_count),
        out_shape=(
            jax.ShapeDtypeStruct((LIVE, own_rows, occ), bf16),
            jax.ShapeDtypeStruct((LIVE,), f32),
        ),
        in_specs=[anywhere, anywhere, vmem, anywhere, anywhere, anywhere, anywhere],
        out_specs=(vmem, vmem),
        scratch_shapes=[
            pltpu.SMEM(counts.shape, jnp.int32),
            pltpu.SMEM(partner.shape, jnp.int32),
            pltpu.VMEM((pairs, chol_count, depth, occ), bf16),
            pltpu.VMEM((slots, own_rows, occ), bf16),
            pltpu.VMEM((depth, occ), bf16),
            pltpu.VMEM((depth, occ), bf16),
            pltpu.VMEM((bit_count, depth, occ), bf16),
            pltpu.VMEM((2 * vectors, rows, orbitals), bf16),
            pltpu.VMEM((slots, occ, occ), bf16),
            pltpu.VMEM((bit_count, occ, occ), bf16),
            pltpu.VMEM((2, field_rows, occ), bf16),
            pltpu.VMEM((bit_count, 2, field_rows, occ), bf16),
            pltpu.VMEM((rows, occ), bf16),
            pltpu.VMEM((pairs, 2 * vectors * rows, occ), f32),
            pltpu.VMEM((pairs, chol_count, own_rows, occ), f32),
            pltpu.VMEM((pairs, 2, own_rows + LOG_ROWS, occ), f32),
            pltpu.VMEM((pairs, own_rows + LOG_ROWS, occ), f32),
            pltpu.VMEM((pairs, others, 2, own_rows + TAIL, occ), bf16),
            pltpu.VMEM((pairs, others, 2, own_rows + TAIL, occ), bf16),
            pltpu.VMEM((LIVE, own_rows, occ), f32),
            pltpu.VMEM((LIVE, LOG_ROWS, occ), f32),
            pltpu.VMEM((own_rows + TAIL, occ), bf16),
            pltpu.VMEM((bit_count, own_rows + TAIL, occ), bf16),
            dma((7 + pairs,)),
            dma((3, bit_count)),
            dma((3, bit_count)),
            dma((1 + chol_count // 2,)),
            dma((1 + chol_count // 2,)),
            dma((pairs,)),
            dma((pairs,)),
            dma((pairs, others, 2)),
            dma((pairs, others, 2)),
            dma((pairs,)),
            dma((pairs,)),
            dma((pairs, others, 2)),
            dma((pairs, others, 2)),
            dma((bit_count,)),
            dma((bit_count,)),
        ],
        compiler_params=pltpu.CompilerParams(
            collective_id=0, has_side_effects=True, vmem_limit_bytes=VMEM_BYTES
        ),
        cost_estimate=pl.CostEstimate(
            flops=2 * slots * vectors * rows * orbitals * occ,
            bytes_accessed=2 * (walkers.size + cholesky.size),
            transcendentals=0,
        ),
    )(*operands)


def solution(mesh):
    in_specs = (
        P("walk", "chol", None),
        P("walk", None, None),
        P("walk", "chol"),
        P("chol", None, None),
        P(),
        P(),
        P(),
    )
    out_specs = (P("walk", "chol", None), P("walk"))
    return jax.shard_map(shards, mesh=mesh, in_specs=in_specs, out_specs=out_specs, check_vma=False)
```
